768 devices in a mesh: gx: 32 (over z_lo, x, core), gy: 24 (over z_hi, y).
Axes of the slice: x: 4, y: 8, z: 12 (z_hi: 3, z_lo: 4; z = z_hi * 4 + z_lo), core: 2. Of those that a mesh axis runs over, the one named last changes fastest.
Arguments:
- start: float32 [19, 64, 192, 128], P(None, 'gx', 'gy'), may hold values from -6 to 6
- adjoint: float32 [19, 64, 192, 128], P(None, 'gx', 'gy'), may hold values from -6 to 6
- solid: int32 [64, 192, 128], P('gx', 'gy'), may hold values 0 or 1
- w_in: float32 [64, 19], replicated, may hold values from -1.25 to 1.25
- b_in: float32 [64], replicated, may hold values from -3 to 3
- w_out: float32 [19, 64], replicated, may hold values from -0.75 to 0.75
- b_out: float32 [19], replicated, may hold values from -1.5 to 1.5
Outputs:
- final_state: float32 [19, 64, 192, 128], P(None, 'gx', 'gy')
- grad_start: float32 [19, 64, 192, 128], P(None, 'gx', 'gy')
- grad_w_in: float32 [64, 19], replicated
- grad_b_in: float32 [64], replicated
- grad_w_out: float32 [19, 64], replicated
- grad_b_out: float32 [19], replicated
The draws below stay inside these ranges and needn't reach their ends.
All inputs are finite; a program needn't handle non-finite values. No bound on the sum of `solid` on one device may be relied on, other than what follows from the above.
Results may differ from the reference program's by a relative error of at most 0.00016.
Values sent between devices are 32-bit elements; how exact they have to be, the bound alone decides.
No kernel may reach another device: no remote copies, remote signals or barrier semaphores. Data moves between devices by JAX's collectives and lax.ppermute only.
A program may use at most 32 MiB of HBM per device.

```python
import math
import jax
import jax.numpy as jnp
from jax import lax

Q = 19
HID = 64
STEPS = 3
NZ = 128
NX = 64
NY = 192
CELLS = 1572864


def touch_ends(result, stream_key, low, high):
    place = [jax.random.randint(jax.random.fold_in(stream_key, axis), (), 0, length) for axis, length in enumerate(result.shape)]
    widest = result.shape.index(max(result.shape))
    beside = place[:widest] + [(place[widest] + 1) % result.shape[widest]] + place[widest + 1:]
    return result.at[tuple(place)].set(low).at[tuple(beside)].set(high)


def levels(stream_key, shape, split, low, high):
    factor_of = 1.0
    for position, shards_of in split:
        steps = jax.random.uniform(jax.random.fold_in(jax.random.fold_in(stream_key, 6), position), (shards_of,), jnp.float32, low / len(split), high / len(split))
        factor_of = factor_of * jnp.repeat(jnp.exp(steps), shape[position] // shards_of).reshape((-1,) + (1,) * (len(shape) - 1 - position))
    return factor_of


def scatter_about(key, shape, width, bound, shards=(), kind=jnp.bfloat16):
    gain = levels(key, shape, shards, -0.22, 0.18) if shards else 1.0
    values = jax.random.normal(key, shape, jnp.float32) * width * gain
    return jnp.minimum(jnp.maximum(values, -bound), bound).astype(kind)


def setup_inputs(seed: int = 0) -> dict:
    arg_keys = jax.random.split(jax.random.key(seed), 8)
    start = scatter_about(arg_keys[0], (Q, NX, NY, NZ), 1.0, 6.0, ((1, 32), (2, 24)), jnp.float32)
    adjoint = scatter_about(arg_keys[1], (Q, NX, NY, NZ), 1.0, 6.0, ((1, 32), (2, 24)), jnp.float32)
    solid = touch_ends((jax.random.randint(arg_keys[2], (NX, NY, NZ), 0, 8) < 1).astype(jnp.int32), jax.random.fold_in(arg_keys[2], 1), 0, 1)
    w_in = scatter_about(arg_keys[3], (HID, Q), Q ** -0.5, 1.25, (), jnp.float32)
    b_in = scatter_about(arg_keys[4], (HID,), 0.5, 3.0, (), jnp.float32)
    w_out = scatter_about(arg_keys[5], (Q, HID), HID ** -0.5, 0.75, (), jnp.float32)
    b_out = scatter_about(arg_keys[6], (Q,), 0.3, 1.5, (), jnp.float32)
    return {"start": start, "adjoint": adjoint, "solid": solid, "w_in": w_in, "b_in": b_in, "w_out": w_out, "b_out": b_out}


velocities = ((0, 0, 0), (1, 0, 0), (-1, 0, 0), (0, 1, 0), (0, -1, 0), (0, 0, 1), (0, 0, -1), (1, 1, 0), (-1, -1, 0), (1, -1, 0), (-1, 1, 0), (1, 0, 1), (-1, 0, -1), (1, 0, -1), (-1, 0, 1), (0, 1, 1), (0, -1, -1), (0, 1, -1), (0, -1, 1))
opposite = (0, 2, 1, 4, 3, 6, 5, 8, 7, 10, 9, 12, 11, 14, 13, 16, 15, 18, 17)

def collide(state, fluid, w_in, b_in, w_out, b_out):
    flat = state.reshape(state.shape[0], -1)
    hidden_units = jnp.tanh(jnp.dot(w_in, flat, precision=lax.Precision.HIGHEST) + b_in[:, None])
    change = jnp.dot(w_out, hidden_units, precision=lax.Precision.HIGHEST) + b_out[:, None]
    return state + fluid * change.reshape(state.shape)

def stream(post_state, solid):
    shifted = jnp.stack([jnp.roll(post_state[number], velocities[number], axis=(0, 1, 2)) for number in range(19)])
    reflected = jnp.stack([shifted[other] for other in opposite])
    return jnp.where(solid[None] == 1, reflected, shifted)

def reference(start, adjoint, solid, w_in, b_in, w_out, b_out):
    fluid = (1 - solid).astype(jnp.float32)[None]
    checked = jax.checkpoint(collide)

    def forward(state, first_w, first_b, second_w, second_b):
        for section in range(STEPS):
            state = stream(checked(state, fluid, first_w, first_b, second_w, second_b), solid)
        return state
    final_state, pullback = jax.vjp(forward, start, w_in, b_in, w_out, b_out)
    grad_start, grad_w_in, grad_b_in, grad_w_out, grad_b_out = pullback(adjoint)
    factor = 1.0 / math.sqrt(CELLS)
    return (final_state, grad_start, grad_w_in * factor, grad_b_in * factor, grad_w_out * factor, grad_b_out * factor)
```

```python
import functools
import math

import jax
import jax.numpy as jnp
from jax import lax
from jax.experimental import pallas as pl
from jax.experimental.pallas import tpu as pltpu
from jax.sharding import PartitionSpec as P

Q = 19
HID = 64
T = 24
ONE = 19
W = 128

velocities = (
    (0, 0, 0),
    (1, 0, 0),
    (-1, 0, 0),
    (0, 1, 0),
    (0, -1, 0),
    (0, 0, 1),
    (0, 0, -1),
    (1, 1, 0),
    (-1, -1, 0),
    (1, -1, 0),
    (-1, 1, 0),
    (1, 0, 1),
    (-1, 0, -1),
    (1, 0, -1),
    (-1, 0, 1),
    (0, 1, 1),
    (0, -1, -1),
    (0, 1, -1),
    (0, -1, 1),
)
opposite = (0, 2, 1, 4, 3, 6, 5, 8, 7, 10, 9, 12, 11, 14, 13, 16, 15, 18, 17)

order = tuple(sorted(range(Q), key=lambda k: -velocities[k][0]))
place = {k: i for i, k in enumerate(order)}
UNITS = 2 * Q + 1
SOLID = 2 * Q


def y_pieces(way):
    pieces = []
    for plane in range(2):
        for k in range(Q):
            pieces.append((plane, place[k], 3 + way * velocities[k][1]))
        for k in range(Q):
            pieces.append((plane, Q + place[k], 2 - way * velocities[k][1]))
        pieces.append((plane, SOLID, 3))
    return pieces


Y_ROWS = 200


def split(a):
    high = a.astype(jnp.bfloat16).astype(jnp.float32)
    return high, a - high


def stack3(high, low):
    parts = [high, low, high]
    if (3 * high.shape[0]) % 16:
        parts.append(jnp.zeros((8, high.shape[1]), jnp.float32))
    return jnp.concatenate(parts, axis=0).astype(jnp.bfloat16)


def weights3(a):
    high, low = split(a)
    parts = [high, high, low]
    if (3 * a.shape[1]) % 16:
        parts.append(jnp.zeros((a.shape[0], 8), jnp.float32))
    return jnp.concatenate(parts, axis=1)


def mm(a, b):
    return lax.dot_general(a, b, (((1,), (0,)), ((), ())), preferred_element_type=jnp.float32)


def mm_t(a, b):
    return lax.dot_general(a, b, (((1,), (1,)), ((), ())), preferred_element_type=jnp.float32)


def load_rows(ref, plane, first, count):
    return jnp.concatenate(
        [ref[plane, (first + i) * T : (first + i + 1) * T, :] for i in range(count)], axis=1
    )


def store_rows(ref, plane, first, count, value):
    for i in range(count):
        ref[plane, (first + i) * T : (first + i + 1) * T, :] = value[:, i * W : (i + 1) * W]


def get8(ref, plane, first, k):
    return ref[plane, pl.ds(first * T + k, 8, stride=T), :]


def put8(ref, plane, first, k, value):
    ref[plane, pl.ds(first * T + k, 8, stride=T), :] = value


def z_shift(value, step):
    if step == 0:
        return value
    return pltpu.roll(value, step % W, axis=1)


def pad_tile():
    row = lax.broadcasted_iota(jnp.int32, (8, W), 0)
    return jnp.where(row == ONE - 16, 1.0, 0.0).astype(jnp.float32)


def pad_rows(ref, plane, first, count):
    tile = pad_tile()
    for i in range(count):
        ref[plane, (first + i) * T + 16 : (first + i + 1) * T, :] = tile


def chunks(count, size):
    return [(i, min(size, count - i)) for i in range(0, count, size)]


def first_kernel(
    start, adjoint, solid, w_in, b_in, w_out, b_out,
    z, to_up, to_down, w1x, w2x, w2tx, w1tx, b2b,
    s0, p1, sq,
):
    sq[...] = jnp.zeros((128, 128), jnp.float32)
    sq[0:HID, 0:Q] = w_in[...]
    a1t = sq[...].T
    sq[...] = a1t
    sq[ONE : ONE + 1, 0:HID] = b_in[...]
    a1t = sq[0:T, 0:HID]
    a1 = sq[...].T[0:HID, 0:T]
    sq[...] = jnp.zeros((128, 128), jnp.float32)
    sq[0:Q, 0:HID] = w_out[...]
    a2 = sq[0:T, 0:HID]
    a2t = sq[...].T[0:HID, 0:T]
    sq[...] = jnp.zeros((128, 128), jnp.float32)
    sq[0:1, 0:Q] = b_out[...]
    b2 = jnp.broadcast_to(sq[...].T[0:T, 0:1], (T, W))
    w1 = weights3(a1)
    w2 = weights3(a2)
    w1x[...] = w1
    w2x[...] = w2
    w2tx[...] = weights3(a2t)
    w1tx[...] = weights3(a1t)
    b2b[...] = b2
    w1 = w1.astype(jnp.bfloat16)
    w2 = w2.astype(jnp.bfloat16)
    for plane in range(2):
        pad_rows(s0, plane, 0, 8)
        for k in range(Q):
            put8(s0, plane, 0, k, start[k, plane])
        sol = solid[plane].astype(jnp.float32)
        z[plane, SOLID, 4:12, :] = sol
        mask = sol > 0.5
        for k in range(Q):
            z[plane, Q + place[k], 4:12, :] = jnp.where(
                mask, adjoint[opposite[k], plane], adjoint[k, plane]
            )
    for plane in range(2):
        for first, count in chunks(8, 4):
            state = load_rows(s0, plane, first, count)
            hidden = jnp.tanh(mm(w1, stack3(*split(state))))
            change = mm(w2, stack3(*split(hidden)))
            for i in range(count):
                y = first + i
                fluid = 1.0 - solid[plane, y : y + 1, :].astype(jnp.float32)
                p1[plane, y * T : (y + 1) * T, :] = state[:, i * W : (i + 1) * W] + fluid * (
                    change[:, i * W : (i + 1) * W] + b2
                )
    for plane in range(2):
        for k in range(Q):
            z[plane, place[k], 4:12, :] = get8(p1, plane, 0, k)
    for ref, way in ((to_up, 1), (to_down, -1)):
        at = 0
        for plane, unit, rows in y_pieces(way):
            begin = 12 - rows if way == 1 else 4
            ref[at : at + rows, :] = z[plane, unit, begin : begin + rows, :]
            at += rows
        ref[at:, :] = jnp.zeros((Y_ROWS - at, W), jnp.float32)


def second_kernel(z_in, from_below, from_above, z, to_right, to_left):
    z[...] = z_in[...]
    for ref, way in ((from_below, 1), (from_above, -1)):
        at = 0
        for plane, unit, rows in y_pieces(way):
            begin = 4 - rows if way == 1 else 12
            z[plane, unit, begin : begin + rows, :] = ref[at : at + rows, :]
            at += rows
    for at, (plane, unit) in enumerate(far_units(1)):
        to_right[at] = z[plane, unit]
    for at, (plane, unit) in enumerate(far_units(-1)):
        to_left[at] = z[plane, unit]


def far_runs(way):
    if way == 1:
        return ((5, 0, 0), (14, 1, 0), (5, 1, Q + 14), (1, 1, SOLID))
    return ((5, 1, 14), (14, 0, 5), (5, 0, Q), (1, 0, SOLID))


def far_units(way):
    return [(plane, first + i) for count, plane, first in far_runs(way) for i in range(count)]


FAR = 25


PLANES = 10
ROWS = 16


def third_kernel(
    scale,
    start, z_own, z_left, z_right, f_left, f_right, w1x, w2x, w2tx, w1tx, b2b,
    final, grad, sums,
    zs, s0, s1, p2, s2, p3, gp, g, acc1, acc2, sems,
):
    copies = [(z_left, zs.at[2:4]), (z_own, zs.at[4:6]), (z_right, zs.at[6:8])]
    for ref, way, base in ((f_left, 1, 0), (f_right, -1, 8)):
        at = 0
        for count, plane, first in far_runs(way):
            copies.append((ref.at[at : at + count], zs.at[base + plane, first : first + count]))
            at += count
    copies = [pltpu.make_async_copy(a, b, sems.at[i]) for i, (a, b) in enumerate(copies)]
    for copy in copies:
        copy.start()

    w1 = w1x[...].astype(jnp.bfloat16)
    w2 = w2x[...].astype(jnp.bfloat16)
    w2t = w2tx[...].astype(jnp.bfloat16)
    w1t = w1tx[...].astype(jnp.bfloat16)
    b2 = b2b[...]
    acc1[...] = jnp.zeros(acc1.shape, jnp.float32)
    acc2[...] = jnp.zeros(acc2.shape, jnp.float32)
    tile = pad_tile()

    def init_pads(ref, planes, first, count):
        for plane in range(planes):
            pad_rows(ref, plane, first, count)

    init_pads(s0, 2, 0, 8)
    for plane in range(2):
        for k in range(Q):
            put8(s0, plane, 0, k, start[k, plane])
    for ref, planes in ((s1, 8), (s2, 6)):
        for plane in range(planes):
            pad_rows(ref, plane, 0, ROWS)
    for plane in range(6):
        for i in range(ROWS):
            gp[plane, i * T + 16 : (i + 1) * T, :] = jnp.zeros((8, W), jnp.float32)

    for copy in copies:
        copy.wait()

    def fluid_rows(x, y):
        return 1.0 - zs[x, SOLID, y : y + 1, :]

    def forward_hidden(state_parts):
        return jnp.tanh(mm(w1, stack3(*state_parts)))

    def collide(p_ref, p_plane, zx, first, count, state, hidden_parts):
        change = mm(w2, stack3(*hidden_parts))
        for i in range(count):
            y = first + i
            p_ref[p_plane, y * T : (y + 1) * T, :] = state[:, i * W : (i + 1) * W] + fluid_rows(
                zx, y
            ) * (change[:, i * W : (i + 1) * W] + b2)

    def backward(own, zx, first, count, state_parts, hidden, hidden_parts, grad_post):
        change = jnp.concatenate(
            [
                fluid_rows(zx, first + i) * grad_post[:, i * W : (i + 1) * W]
                for i in range(count)
            ],
            axis=1,
        )
        change_parts = split(change)
        grad_hidden = mm(w2t, stack3(*change_parts))
        grad_pre = grad_hidden * (1.0 - hidden * hidden)
        pre_parts = split(grad_pre)
        back = grad_post + mm(w1t, stack3(*pre_parts))
        low = max(first, 4)
        high = min(first + count, 12)

        if own and high > low:
            part = slice((low - first) * W, (high - first) * W)
            left = jnp.concatenate([a[:, part] for a in state_parts], axis=0)
            right = jnp.concatenate([a[:, part] for a in pre_parts + change_parts], axis=0)
            acc1[...] += mm_t(left.astype(jnp.bfloat16), right.astype(jnp.bfloat16))
            left = jnp.concatenate([a[:, part] for a in change_parts], axis=0)
            right = jnp.concatenate([a[:, part] for a in hidden_parts], axis=0)
            acc2[...] += mm_t(left.astype(jnp.bfloat16), right.astype(jnp.bfloat16))
        return back

    def over_planes(halo, body):
        if halo:
            lax.fori_loop(
                0,
                2 * halo,
                lambda i, c: body(False, jnp.where(i < halo, i, i + 2), c),
                0,
            )
        lax.fori_loop(0, 2, lambda i, c: body(True, i + halo, c), 0)

    def reflect(values, mask):
        return [jnp.where(mask, values[opposite[k]], values[k]) for k in range(Q)]

    def stage1(j, carry):
        zx = j + 1
        for y in (1, 7):
            moved = []
            for k in range(Q):
                cx, cy, cz = velocities[k]
                moved.append(z_shift(zs[zx - cx, place[k], y - cy : y - cy + 8, :], cz))
            moved = reflect(moved, zs[zx, SOLID, y : y + 8, :] > 0.5)
            for k in range(Q):
                put8(s1, j, y, k, moved[k])
        for first, count in chunks(14, 4):
            first += 1
            state = load_rows(s1, j, first, count)
            hidden = forward_hidden(split(state))
            collide(p2, j, zx, first, count, state, split(hidden))
        return carry

    lax.fori_loop(0, 8, stage1, 0)

    def stage2(own, j, carry):
        zx = j + 2
        for y in (2, 6):
            moved = []
            for k in range(Q):
                cx, cy, cz = velocities[k]
                moved.append(z_shift(get8(p2, j + 1 - cx, y - cy, k), cz))
            moved = reflect(moved, zs[zx, SOLID, y : y + 8, :] > 0.5)
            for k in range(Q):
                put8(s2, j, y, k, moved[k])
            for k in range(Q):
                cx, cy, cz = velocities[k]
                value = zs[zx + cx, Q + place[k], y + cy : y + cy + 8, :]
                put8(gp, j, y, k, z_shift(value, -cz))
        for first, count in chunks(12, 4):
            first += 2
            state = load_rows(s2, j, first, count)
            state_parts = split(state)
            hidden = forward_hidden(state_parts)
            hidden_parts = split(hidden)
            collide(p3, j, zx, first, count, state, hidden_parts)
            grad_post = load_rows(gp, j, first, count)
            back = backward(own, zx, first, count, state_parts, hidden, hidden_parts, grad_post)
            store_rows(g, j, first, count, back)
        return carry

    over_planes(2, stage2)

    for plane in range(2):
        moved = []
        for k in range(Q):
            cx, cy, cz = velocities[k]
            moved.append(z_shift(get8(p3, plane + 2 - cx, 4 - cy, k), cz))
        moved = reflect(moved, zs[plane + 4, SOLID, 4:12, :] > 0.5)
        for k in range(Q):
            final[k, plane] = moved[k]

    def run_back(g_ref, g_plane, zx, y, out_plane):
        for k in range(Q):
            cx, cy, cz = velocities[k]
            one = get8(g_ref, g_plane + cx, y + cy, k)
            if k != 0:
                other = get8(g_ref, g_plane + cx, y + cy, opposite[k])
                mask = zs[zx + cx, SOLID, y + cy : y + cy + 8, :] > 0.5
                one = jnp.where(mask, other, one)
            put8(gp, out_plane, y, k, z_shift(one, -cz))

    def stage3(own, j, carry):
        zx = j + 3
        for y in (3, 5):
            run_back(g, j + 1, zx, y, j)
        for first, count in ((3, 5), (8, 5)):
            state_parts = split(load_rows(s1, j + 2, first, count))
            hidden = forward_hidden(state_parts)
            grad_post = load_rows(gp, j, first, count)
            back = backward(own, zx, first, count, state_parts, hidden, split(hidden), grad_post)
            store_rows(p2, j, first, count, back)
        return carry

    over_planes(1, stage3)

    def stage4(own, j, carry):
        zx = j + 4
        run_back(p2, j + 1, zx, 4, j)
        for first, count in ((4, 4), (8, 4)):
            state_parts = split(load_rows(s0, j, first - 4, count))
            hidden = forward_hidden(state_parts)
            grad_post = load_rows(gp, j, first, count)
            back = backward(own, zx, first, count, state_parts, hidden, split(hidden), grad_post)
            store_rows(g, j, first, count, back)
        for k in range(Q):
            grad[k, j] = get8(g, j, 4, k)
        return carry

    over_planes(0, stage4)

    one = acc1[0:T, :] + acc1[T : 2 * T, :]
    two = acc2[0:T, :] + acc2[T : 2 * T, :]
    in_part = one[:, 0:HID] + one[:, HID : 2 * HID]
    out_part = two[:, 0:HID] + two[:, HID : 2 * HID]
    bias = one[:, 2 * HID : 2 * HID + T] + one[:, 2 * HID + T : 2 * HID + 2 * T]
    sums[...] = jnp.zeros(sums.shape, jnp.float32)
    sums[0:T, 0:HID] = in_part * scale
    sums[0:Q, HID : 2 * HID] = out_part[0:Q, :] * scale
    sums[ONE : ONE + 1, HID : HID + T] = bias[ONE : ONE + 1, :] * scale


def shift(x, axis, step):
    count = lax.axis_size(axis)
    return lax.ppermute(x, axis, [(i, (i + step) % count) for i in range(count)])


def spread(x, axis):
    count = lax.axis_size(axis)
    return lax.all_to_all(jnp.broadcast_to(x[None], (count,) + x.shape), axis, 0, 0)


F32 = jnp.float32


def shape(*dims):
    return jax.ShapeDtypeStruct(dims, F32)


PARAMS = pltpu.CompilerParams(vmem_limit_bytes=48 * 1024 * 1024)


def on_device(start, adjoint, solid, w_in, b_in, w_out, b_out):
    rows = pltpu.VMEM
    z, to_up, to_down, w1x, w2x, w2tx, w1tx, b2b = pl.pallas_call(
        first_kernel,
        out_shape=(
            shape(2, UNITS, ROWS, W),
            shape(Y_ROWS, W),
            shape(Y_ROWS, W),
            shape(HID, 80),
            shape(T, 192),
            shape(HID, 80),
            shape(T, 192),
            shape(T, W),
        ),
        scratch_shapes=[
            rows((2, 8 * T, W), F32),
            rows((2, 8 * T, W), F32),
            rows((128, 128), F32),
        ],
        compiler_params=PARAMS,
        name="first",
    )(start, adjoint, solid, w_in, b_in.reshape(1, HID), w_out, b_out.reshape(1, Q))

    from_below = shift(to_up, "gy", 1)
    from_above = shift(to_down, "gy", -1)

    z, to_right, to_left = pl.pallas_call(
        second_kernel,
        out_shape=(shape(2, UNITS, ROWS, W), shape(FAR, ROWS, W), shape(FAR, ROWS, W)),
        compiler_params=PARAMS,
        name="second",
    )(z, from_below, from_above)

    z_left = shift(z, "gx", 1)
    z_right = shift(z, "gx", -1)
    f_left = shift(to_right, "gx", 2)
    f_right = shift(to_left, "gx", -2)

    cells = 16 * W * lax.axis_size("gx") * lax.axis_size("gy")
    vmem = pl.BlockSpec(memory_space=pltpu.VMEM)
    hbm = pl.BlockSpec(memory_space=pl.ANY)
    final, grad, sums = pl.pallas_call(
        functools.partial(third_kernel, 1.0 / math.sqrt(cells)),
        out_shape=(shape(Q, 2, 8, W), shape(Q, 2, 8, W), shape(T, W)),
        in_specs=[vmem] + [hbm] * 5 + [vmem] * 5,
        scratch_shapes=[
            rows((PLANES, UNITS, ROWS, W), F32),
            rows((2, 8 * T, W), F32),
            rows((8, ROWS * T, W), F32),
            rows((8, ROWS * T, W), F32),
            rows((6, ROWS * T, W), F32),
            rows((6, ROWS * T, W), F32),
            rows((6, ROWS * T, W), F32),
            rows((6, ROWS * T, W), F32),
            rows((2 * T, 2 * HID + 2 * T), F32),
            rows((2 * T, 2 * HID), F32),
            pltpu.SemaphoreType.DMA((11,)),
        ],
        compiler_params=PARAMS,
        name="third",
    )(start, z, z_left, z_right, f_left, f_right, w1x, w2x, w2tx, w1tx, b2b)

    parts = lax.axis_size("gx")
    used = (ONE + 1) * W
    share = -(-used // parts)
    flat = jnp.pad(sums[0 : ONE + 1].reshape(-1), (0, share * parts - used))
    mine = lax.all_to_all(flat.reshape(parts, share), "gx", 0, 0).sum(0)
    mine = spread(mine, "gy").sum(0)
    total = spread(mine, "gx").reshape(-1)[:used].reshape(ONE + 1, W)
    return (
        final,
        grad,
        total[0:Q, 0:HID].T,
        total[ONE, 0:HID],
        total[0:Q, HID : 2 * HID],
        total[ONE, HID : HID + Q],
    )


def solution(mesh):
    return jax.shard_map(
        on_device,
        mesh=mesh,
        in_specs=(
            P(None, "gx", "gy", None),
            P(None, "gx", "gy", None),
            P("gx", "gy", None),
            P(),
            P(),
            P(),
            P(),
        ),
        out_specs=(P(None, "gx", "gy", None), P(None, "gx", "gy", None), P(), P(), P(), P()),
        check_vma=False,
    )
```

```python
import functools
import math

import jax
import jax.numpy as jnp
from jax import lax
from jax.experimental import pallas as pl
from jax.experimental.pallas import tpu as pltpu
from jax.sharding import PartitionSpec as P

Q = 19
HID = 64
T = 24
ONE = 19
W = 128

velocities = (
    (0, 0, 0),
    (1, 0, 0),
    (-1, 0, 0),
    (0, 1, 0),
    (0, -1, 0),
    (0, 0, 1),
    (0, 0, -1),
    (1, 1, 0),
    (-1, -1, 0),
    (1, -1, 0),
    (-1, 1, 0),
    (1, 0, 1),
    (-1, 0, -1),
    (1, 0, -1),
    (-1, 0, 1),
    (0, 1, 1),
    (0, -1, -1),
    (0, 1, -1),
    (0, -1, 1),
)
opposite = (0, 2, 1, 4, 3, 6, 5, 8, 7, 10, 9, 12, 11, 14, 13, 16, 15, 18, 17)

order = tuple(sorted(range(Q), key=lambda k: -velocities[k][0]))
place = {k: i for i, k in enumerate(order)}
UNITS = 2 * Q + 1
SOLID = 2 * Q


def y_pieces(way):
    pieces = []
    for plane in range(2):
        for k in range(Q):
            pieces.append((plane, place[k], 3 + way * velocities[k][1]))
        for k in range(Q):
            pieces.append((plane, Q + place[k], 2 - way * velocities[k][1]))
        pieces.append((plane, SOLID, 3))
    return pieces


Y_ROWS = 200


def split(a):
    high = a.astype(jnp.bfloat16).astype(jnp.float32)
    return high, a - high


def stack3(high, low):
    parts = [high, low, high]
    if (3 * high.shape[0]) % 16:
        parts.append(jnp.zeros((8, high.shape[1]), jnp.float32))
    return jnp.concatenate(parts, axis=0).astype(jnp.bfloat16)


def weights3(a):
    high, low = split(a)
    parts = [high, high, low]
    if (3 * a.shape[1]) % 16:
        parts.append(jnp.zeros((a.shape[0], 8), jnp.float32))
    return jnp.concatenate(parts, axis=1)


def weights2(a):
    high, low = split(a)
    top = jnp.concatenate([high, high], axis=1)
    bottom = jnp.concatenate([low, jnp.zeros_like(low)], axis=1)
    return jnp.concatenate([top, bottom], axis=0)


def mm2(weights, parts):
    both = mm(weights, jnp.concatenate(parts, axis=0).astype(jnp.bfloat16))
    return both[0:T] + both[T:]


def mm(a, b):
    return lax.dot_general(a, b, (((1,), (0,)), ((), ())), preferred_element_type=jnp.float32)


def mm_t(a, b):
    return lax.dot_general(a, b, (((1,), (1,)), ((), ())), preferred_element_type=jnp.float32)


def load_rows(ref, plane, first, count):
    return jnp.concatenate(
        [ref[plane, (first + i) * T : (first + i + 1) * T, :] for i in range(count)], axis=1
    )


def store_rows(ref, plane, first, count, value):
    for i in range(count):
        ref[plane, (first + i) * T : (first + i + 1) * T, :] = value[:, i * W : (i + 1) * W]


def get8(ref, plane, first, k):
    return ref[plane, pl.ds(first * T + k, 8, stride=T), :]


def put8(ref, plane, first, k, value):
    ref[plane, pl.ds(first * T + k, 8, stride=T), :] = value


def z_shift(value, step):
    if step == 0:
        return value
    return pltpu.roll(value, step % W, axis=1)


def pad_tile():
    row = lax.broadcasted_iota(jnp.int32, (8, W), 0)
    return jnp.where(row == ONE - 16, 1.0, 0.0).astype(jnp.float32)


def pad_rows(ref, plane, first, count):
    tile = pad_tile()
    for i in range(count):
        ref[plane, (first + i) * T + 16 : (first + i + 1) * T, :] = tile


def chunks(count, size):
    return [(i, min(size, count - i)) for i in range(0, count, size)]


def first_kernel(
    start_hbm, adjoint_hbm, solid_hbm, w_in_t_hbm, b_in_hbm, w_out_hbm, b_out_hbm,
    z, to_even, to_odd, s0, w1x, w2x, w2tx, w1tx, b2b,
    p1, sq, start, adjoint, solid, w_in_t, b_in, w_out, b_out, sems,
):
    pairs = (
        (w_in_t_hbm, w_in_t), (b_in_hbm, b_in), (w_out_hbm, w_out), (b_out_hbm, b_out),
        (start_hbm, start), (solid_hbm, solid), (adjoint_hbm, adjoint),
    )
    copies = [pltpu.make_async_copy(a, b, sems.at[i]) for i, (a, b) in enumerate(pairs)]
    for copy in copies:
        copy.start()
    sq[...] = jnp.zeros((128, 128), jnp.float32)
    for plane in range(2):
        pad_rows(s0, plane, 0, 8)
    for copy in copies[:4]:
        copy.wait()
    sq[0:Q, 0:HID] = w_in_t[...]
    sq[ONE : ONE + 1, 0:HID] = b_in[...]
    a1t = sq[0:T, 0:HID]
    a1 = sq[...].T[0:HID, 0:T]
    sq[...] = jnp.zeros((128, 128), jnp.float32)
    sq[0:Q, 0:HID] = w_out[...]
    a2 = sq[0:T, 0:HID]
    a2t = sq[...].T[0:HID, 0:T]
    sq[...] = jnp.zeros((128, 128), jnp.float32)
    sq[0:1, 0:Q] = b_out[...]
    b2 = jnp.broadcast_to(sq[...].T[0:T, 0:1], (T, W))
    w1 = weights3(a1)
    w2 = weights2(a2)
    w1x[...] = w1
    w2x[...] = w2
    w2tx[...] = weights3(a2t)
    w1tx[...] = weights2(a1t)
    b2b[...] = b2
    w1 = w1.astype(jnp.bfloat16)
    w2 = w2.astype(jnp.bfloat16)
    for copy in copies[4:]:
        copy.wait()
    for plane in range(2):
        for k in range(Q):
            put8(s0, plane, 0, k, start[k, plane])
        sol = solid[plane].astype(jnp.float32)
        z[plane, SOLID, 4:12, :] = sol
        mask = sol > 0.5
        for k in range(Q):
            z[plane, Q + place[k], 4:12, :] = jnp.where(
                mask, adjoint[opposite[k], plane], adjoint[k, plane]
            )
    state = jnp.concatenate([load_rows(s0, plane, 0, 8) for plane in range(2)], axis=1)
    hidden = jnp.tanh(mm(w1, stack3(*split(state))))
    change = mm2(w2, split(hidden))
    for i in range(16):
        plane, y = divmod(i, 8)
        fluid = 1.0 - solid[plane, y : y + 1, :].astype(jnp.float32)
        p1[plane, y * T : (y + 1) * T, :] = state[:, i * W : (i + 1) * W] + fluid * (
            change[:, i * W : (i + 1) * W] + b2
        )
    for plane in range(2):
        for k in range(Q):
            z[plane, place[k], 4:12, :] = get8(p1, plane, 0, k)

    def pack(ref, way):
        at = 0
        for plane, unit, rows in y_pieces(way):
            begin = 12 - rows if way == 1 else 4
            ref[at : at + rows, :] = z[plane, unit, begin : begin + rows, :]
            at += rows
        ref[at:, :] = jnp.zeros((Y_ROWS - at, W), jnp.float32)

    odd = lax.rem(lax.axis_index("gy"), 2)

    @pl.when(odd == 0)
    def _():
        pack(to_even, 1)
        pack(to_odd, -1)

    @pl.when(odd == 1)
    def _():
        pack(to_even, -1)
        pack(to_odd, 1)


def second_kernel(z_in, from_even, from_odd, z, to_near, to_far):
    z[...] = z_in[...]

    def unpack(ref, way):
        at = 0
        for plane, unit, rows in y_pieces(way):
            begin = 4 - rows if way == 1 else 12
            z[plane, unit, begin : begin + rows, :] = ref[at : at + rows, :]
            at += rows

    odd = lax.rem(lax.axis_index("gy"), 2)

    @pl.when(odd == 0)
    def _():
        unpack(from_even, -1)
        unpack(from_odd, 1)

    @pl.when(odd == 1)
    def _():
        unpack(from_even, 1)
        unpack(from_odd, -1)

    def pack(ref, way):
        at = 0
        for count, plane, first in far_runs(way):
            ref[at : at + count] = z[plane, first : first + count]
            at += count

    low = lax.rem(lax.axis_index("gx"), 4) < 2

    @pl.when(low)
    def _():
        pack(to_near, 1)
        pack(to_far, -1)

    @pl.when(jnp.logical_not(low))
    def _():
        pack(to_near, -1)
        pack(to_far, 1)


def far_runs(way):
    if way == 1:
        return ((5, 0, 0), (14, 1, 0), (5, 1, Q + 14), (1, 1, SOLID))
    return ((5, 1, 14), (14, 0, 5), (5, 0, Q), (1, 0, SOLID))


FAR = 25


PLANES = 10
ROWS = 16


def third_kernel(
    scale,
    s0, z_own, z_even, z_odd, f_near, f_far, w1x, w2x, w2tx, w1tx, b2b,
    final, grad, sums,
    zs, s1, p2, s2, p3, gp, g, acc1, acc2, sems,
):
    index = lax.axis_index("gx")
    odd = lax.rem(index, 2)
    high = lax.rem(index, 4) // 2
    copies = [
        (z_even, zs.at[pl.ds(6 - 4 * odd, 2)]),
        (z_own, zs.at[4:6]),
        (z_odd, zs.at[pl.ds(2 + 4 * odd, 2)]),
    ]
    for ref, left in ((f_near, high), (f_far, 1 - high)):
        at = 0
        for (count, plane, first), (_, plane_r, first_r) in zip(far_runs(1), far_runs(-1)):
            plane_r += 8
            x = plane_r + left * (plane - plane_r)
            unit = first_r + left * (first - first_r)
            copies.append((ref.at[at : at + count], zs.at[x, pl.ds(unit, count)]))
            at += count
    copies = [pltpu.make_async_copy(a, b, sems.at[i]) for i, (a, b) in enumerate(copies)]
    for copy in copies:
        copy.start()

    w1 = w1x[...].astype(jnp.bfloat16)
    w2 = w2x[...].astype(jnp.bfloat16)
    w2t = w2tx[...].astype(jnp.bfloat16)
    w1t = w1tx[...].astype(jnp.bfloat16)
    b2 = b2b[...]
    acc1[...] = jnp.zeros(acc1.shape, jnp.float32)
    acc2[...] = jnp.zeros(acc2.shape, jnp.float32)
    for ref, planes in ((s1, 8), (s2, 6)):
        for plane in range(planes):
            pad_rows(ref, plane, 0, ROWS)
    for plane in range(6):
        for i in range(ROWS):
            gp[plane, i * T + 16 : (i + 1) * T, :] = jnp.zeros((8, W), jnp.float32)

    for copy in copies:
        copy.wait()

    def fluid_rows(x, y):
        return 1.0 - zs[x, SOLID, y : y + 1, :]

    def forward_hidden(state_parts):
        return jnp.tanh(mm(w1, stack3(*state_parts)))

    def collide(p_ref, p_plane, zx, first, count, state, hidden_parts):
        change = mm2(w2, hidden_parts)
        for i in range(count):
            y = first + i
            p_ref[p_plane, y * T : (y + 1) * T, :] = state[:, i * W : (i + 1) * W] + fluid_rows(
                zx, y
            ) * (change[:, i * W : (i + 1) * W] + b2)

    def backward(own, zx, first, count, state_parts, hidden, hidden_parts, grad_post):
        change = jnp.concatenate(
            [
                fluid_rows(zx, first + i) * grad_post[:, i * W : (i + 1) * W]
                for i in range(count)
            ],
            axis=1,
        )
        change_parts = split(change)
        grad_hidden = mm(w2t, stack3(*change_parts))
        grad_pre = grad_hidden * (1.0 - hidden * hidden)
        pre_parts = split(grad_pre)
        back = grad_post + mm2(w1t, pre_parts)
        low = max(first, 4)
        high = min(first + count, 12)

        if own and high > low:
            part = slice((low - first) * W, (high - first) * W)
            left = jnp.concatenate([a[:, part] for a in state_parts], axis=0)
            right = jnp.concatenate([a[:, part] for a in pre_parts + change_parts], axis=0)
            acc1[...] += mm_t(left.astype(jnp.bfloat16), right.astype(jnp.bfloat16))
            left = jnp.concatenate([a[:, part] for a in change_parts], axis=0)
            right = jnp.concatenate([a[:, part] for a in hidden_parts], axis=0)
            acc2[...] += mm_t(left.astype(jnp.bfloat16), right.astype(jnp.bfloat16))
        return back

    def over_planes(halo, body):
        if halo:
            lax.fori_loop(
                0,
                2 * halo,
                lambda i, c: body(False, jnp.where(i < halo, i, i + 2), c),
                0,
                unroll=2 * halo,
            )
        lax.fori_loop(0, 2, lambda i, c: body(True, i + halo, c), 0, unroll=2)

    def reflect(values, mask):
        return [jnp.where(mask, values[opposite[k]], values[k]) for k in range(Q)]

    def stage1(j, carry):
        zx = j + 1
        for y in (1, 7):
            moved = []
            for k in range(Q):
                cx, cy, cz = velocities[k]
                moved.append(z_shift(zs[zx - cx, place[k], y - cy : y - cy + 8, :], cz))
            moved = reflect(moved, zs[zx, SOLID, y : y + 8, :] > 0.5)
            for k in range(Q):
                put8(s1, j, y, k, moved[k])
        for first, count in chunks(14, 14):
            first += 1
            state = load_rows(s1, j, first, count)
            hidden = forward_hidden(split(state))
            collide(p2, j, zx, first, count, state, split(hidden))
        return carry

    lax.fori_loop(0, 8, stage1, 0, unroll=8)

    def stage2(own, j, carry):
        zx = j + 2
        for y in (2, 6):
            moved = []
            for k in range(Q):
                cx, cy, cz = velocities[k]
                moved.append(z_shift(get8(p2, j + 1 - cx, y - cy, k), cz))
            moved = reflect(moved, zs[zx, SOLID, y : y + 8, :] > 0.5)
            for k in range(Q):
                put8(s2, j, y, k, moved[k])
            for k in range(Q):
                cx, cy, cz = velocities[k]
                value = zs[zx + cx, Q + place[k], y + cy : y + cy + 8, :]
                put8(gp, j, y, k, z_shift(value, -cz))
        for first, count in chunks(12, 12):
            first += 2
            state = load_rows(s2, j, first, count)
            state_parts = split(state)
            hidden = forward_hidden(state_parts)
            hidden_parts = split(hidden)
            collide(p3, j, zx, first, count, state, hidden_parts)
            grad_post = load_rows(gp, j, first, count)
            back = backward(own, zx, first, count, state_parts, hidden, hidden_parts, grad_post)
            store_rows(g, j, first, count, back)
        return carry

    over_planes(2, stage2)

    for plane in range(2):
        moved = []
        for k in range(Q):
            cx, cy, cz = velocities[k]
            moved.append(z_shift(get8(p3, plane + 2 - cx, 4 - cy, k), cz))
        moved = reflect(moved, zs[plane + 4, SOLID, 4:12, :] > 0.5)
        for k in range(Q):
            final[k, plane] = moved[k]

    def run_back(g_ref, g_plane, zx, y, out_plane):
        for k in range(Q):
            cx, cy, cz = velocities[k]
            one = get8(g_ref, g_plane + cx, y + cy, k)
            if k != 0:
                other = get8(g_ref, g_plane + cx, y + cy, opposite[k])
                mask = zs[zx + cx, SOLID, y + cy : y + cy + 8, :] > 0.5
                one = jnp.where(mask, other, one)
            put8(gp, out_plane, y, k, z_shift(one, -cz))

    def stage3(own, j, carry):
        zx = j + 3
        for y in (3, 5):
            run_back(g, j + 1, zx, y, j)
        for first, count in ((3, 10),):
            state_parts = split(load_rows(s1, j + 2, first, count))
            hidden = forward_hidden(state_parts)
            grad_post = load_rows(gp, j, first, count)
            back = backward(own, zx, first, count, state_parts, hidden, split(hidden), grad_post)
            store_rows(p2, j, first, count, back)
        return carry

    over_planes(1, stage3)

    def stage4(own, j, carry):
        zx = j + 4
        run_back(p2, j + 1, zx, 4, j)
        for first, count in ((4, 8),):
            state_parts = split(load_rows(s0, j, first - 4, count))
            hidden = forward_hidden(state_parts)
            grad_post = load_rows(gp, j, first, count)
            back = backward(own, zx, first, count, state_parts, hidden, split(hidden), grad_post)
            store_rows(g, j, first, count, back)
        for k in range(Q):
            grad[k, j] = get8(g, j, 4, k)
        return carry

    over_planes(0, stage4)

    one = acc1[0:T, :] + acc1[T : 2 * T, :]
    two = acc2[0:T, :] + acc2[T : 2 * T, :]
    in_part = one[:, 0:HID] + one[:, HID : 2 * HID]
    out_part = two[:, 0:HID] + two[:, HID : 2 * HID]
    bias = one[:, 2 * HID : 2 * HID + T] + one[:, 2 * HID + T : 2 * HID + 2 * T]
    sums[...] = jnp.zeros(sums.shape, jnp.float32)
    sums[0:T, 0:HID] = in_part * scale
    sums[0:Q, HID : 2 * HID] = out_part[0:Q, :] * scale
    sums[ONE : ONE + 1, HID : HID + T] = bias[ONE : ONE + 1, :] * scale


def last_kernel(parts, grad_w_in_t, grad_b_in, grad_w_out, grad_b_out):
    total = parts[0]
    for i in range(1, parts.shape[0]):
        total = total + parts[i]
    grad_w_in_t[...] = total[0:Q, 0:HID]
    grad_b_in[...] = total[ONE : ONE + 1, 0:HID]
    grad_w_out[...] = total[0:Q, HID : 2 * HID]
    grad_b_out[...] = total[ONE : ONE + 1, HID : HID + Q]


def swap_even(x, axis, step=1):
    count = lax.axis_size(axis)
    return lax.ppermute(x, axis, [(i, i ^ step) for i in range(count)])


def swap_odd(x, axis, step=1):
    count = lax.axis_size(axis)
    return lax.ppermute(
        x, axis, [(i, (i + step if i & step else i - step) % count) for i in range(count)]
    )


def spread(x, groups):
    count = len(groups[0])
    return lax.all_to_all(
        jnp.broadcast_to(x[None], (count,) + x.shape), ("gx", "gy"), 0, 0, axis_index_groups=groups
    )


def sum_groups():
    gx, gy = lax.axis_size("gx"), lax.axis_size("gy")
    nx, ny = math.gcd(gx, 8), math.gcd(gy, 8)
    zs = [(a, b) for b in range(gy // ny) for a in range(gx // nx)]

    def at(z, x, y):
        return (z[0] * nx + x) * gy + z[1] * ny + y

    return (
        [[at(z, x, y) for x in range(nx)] for z in zs for y in range(ny)],
        [[at(z, x, y) for z in zs] for x in range(nx) for y in range(ny)],
        [[at(z, x, y) for y in range(ny)] for z in zs for x in range(nx)],
    )


F32 = jnp.float32


def shape(*dims):
    return jax.ShapeDtypeStruct(dims, F32)


FIRST_VMEM = 63 * 1024 * 1024
PARAMS = pltpu.CompilerParams(vmem_limit_bytes=48 * 1024 * 1024)


def on_device(start, adjoint, solid, w_in, b_in, w_out, b_out):
    rows = pltpu.VMEM
    z, to_even, to_odd, s0, w1x, w2x, w2tx, w1tx, b2b = pl.pallas_call(
        first_kernel,
        out_shape=(
            shape(2, UNITS, ROWS, W),
            shape(Y_ROWS, W),
            shape(Y_ROWS, W),
            shape(2, 8 * T, W),
            shape(HID, 80),
            shape(2 * T, 2 * HID),
            shape(HID, 80),
            shape(2 * T, 2 * HID),
            shape(T, W),
        ),
        in_specs=[pl.BlockSpec(memory_space=pltpu.HBM)] * 7,
        scratch_shapes=[
            rows((2, 8 * T, W), F32),
            rows((128, 128), F32),
            rows((Q, 2, 8, W), F32),
            rows((Q, 2, 8, W), F32),
            rows((2, 8, W), jnp.int32),
            rows((Q, HID), F32),
            rows((1, HID), F32),
            rows((Q, HID), F32),
            rows((1, Q), F32),
            pltpu.SemaphoreType.DMA((7,)),
        ],
        compiler_params=pltpu.CompilerParams(vmem_limit_bytes=FIRST_VMEM),
        name="first",
    )(start, adjoint, solid, w_in.T, b_in.reshape(1, HID), w_out, b_out.reshape(1, Q))

    from_even = swap_even(to_even, "gy")
    from_odd = swap_odd(to_odd, "gy")

    z, to_near, to_far = pl.pallas_call(
        second_kernel,
        out_shape=(shape(2, UNITS, ROWS, W), shape(FAR, ROWS, W), shape(FAR, ROWS, W)),
        compiler_params=PARAMS,
        name="second",
    )(z, from_even, from_odd)

    z_odd = swap_odd(z, "gx")
    f_far = swap_odd(to_far, "gx", 2)
    f_near = swap_even(to_near, "gx", 2)
    z_even = swap_even(z, "gx")

    cells = 16 * W * lax.axis_size("gx") * lax.axis_size("gy")
    vmem = pl.BlockSpec(memory_space=pltpu.VMEM)
    hbm = pl.BlockSpec(memory_space=pl.ANY)
    final, grad, sums = pl.pallas_call(
        functools.partial(third_kernel, 1.0 / math.sqrt(cells)),
        out_shape=(shape(Q, 2, 8, W), shape(Q, 2, 8, W), shape(T, W)),
        in_specs=[vmem] + [hbm] * 5 + [vmem] * 5,
        scratch_shapes=[
            rows((PLANES, UNITS, ROWS, W), F32),
            rows((8, ROWS * T, W), F32),
            rows((8, ROWS * T, W), F32),
            rows((6, ROWS * T, W), F32),
            rows((6, ROWS * T, W), F32),
            rows((6, ROWS * T, W), F32),
            rows((6, ROWS * T, W), F32),
            rows((2 * T, 2 * HID + 2 * T), F32),
            rows((2 * T, 2 * HID), F32),
            pltpu.SemaphoreType.DMA((11,)),
        ],
        compiler_params=PARAMS,
        name="third",
    )(s0, z, z_even, z_odd, f_near, f_far, w1x, w2x, w2tx, w1tx, b2b)

    along_x, along_z, along_y = sum_groups()
    sums = spread(sums, along_x).sum(0)
    sums = spread(sums, along_z).sum(0)
    grad_w_in_t, grad_b_in, grad_w_out, grad_b_out = pl.pallas_call(
        last_kernel,
        out_shape=(shape(Q, HID), shape(1, HID), shape(Q, HID), shape(1, Q)),
        compiler_params=PARAMS,
        name="last",
    )(spread(sums, along_y))
    return final, grad, grad_w_in_t.T, grad_b_in[0], grad_w_out, grad_b_out[0]


def solution(mesh):
    return jax.shard_map(
        on_device,
        mesh=mesh,
        in_specs=(
            P(None, "gx", "gy", None),
            P(None, "gx", "gy", None),
            P("gx", "gy", None),
            P(),
            P(),
            P(),
            P(),
        ),
        out_specs=(P(None, "gx", "gy", None), P(None, "gx", "gy", None), P(), P(), P(), P()),
        check_vma=False,
    )
```

```python
import functools
import math

import jax
import jax.numpy as jnp
from jax import lax
from jax.experimental import pallas as pl
from jax.experimental.pallas import tpu as pltpu
from jax.sharding import PartitionSpec as P

Q = 19
HID = 64
T = 24
ONE = 19
W = 128

velocities = (
    (0, 0, 0),
    (1, 0, 0),
    (-1, 0, 0),
    (0, 1, 0),
    (0, -1, 0),
    (0, 0, 1),
    (0, 0, -1),
    (1, 1, 0),
    (-1, -1, 0),
    (1, -1, 0),
    (-1, 1, 0),
    (1, 0, 1),
    (-1, 0, -1),
    (1, 0, -1),
    (-1, 0, 1),
    (0, 1, 1),
    (0, -1, -1),
    (0, 1, -1),
    (0, -1, 1),
)
opposite = (0, 2, 1, 4, 3, 6, 5, 8, 7, 10, 9, 12, 11, 14, 13, 16, 15, 18, 17)

order = tuple(sorted(range(Q), key=lambda k: -velocities[k][0]))
place = {k: i for i, k in enumerate(order)}
UNITS = 2 * Q + 1
SOLID = 2 * Q


def y_pieces(way):
    pieces = []
    for plane in range(2):
        for k in range(Q):
            pieces.append((plane, place[k], 3 + way * velocities[k][1]))
        for k in range(Q):
            pieces.append((plane, Q + place[k], 2 - way * velocities[k][1]))
        pieces.append((plane, SOLID, 3))
    return pieces


Y_ROWS = 200


def split(a):
    high = a.astype(jnp.bfloat16).astype(jnp.float32)
    return high, a - high


def stack3(high, low):
    parts = [high, low, high]
    if (3 * high.shape[0]) % 16:
        parts.append(jnp.zeros((8, high.shape[1]), jnp.float32))
    return jnp.concatenate(parts, axis=0).astype(jnp.bfloat16)


def weights3(a):
    high, low = split(a)
    parts = [high, high, low]
    if (3 * a.shape[1]) % 16:
        parts.append(jnp.zeros((a.shape[0], 8), jnp.float32))
    return jnp.concatenate(parts, axis=1)


def weights2(a):
    high, low = split(a)
    top = jnp.concatenate([high, high], axis=1)
    bottom = jnp.concatenate([low, jnp.zeros_like(low)], axis=1)
    return jnp.concatenate([top, bottom], axis=0)


def mm2(weights, parts):
    both = mm(weights, jnp.concatenate(parts, axis=0).astype(jnp.bfloat16))
    return both[0:T] + both[T:]


def mm(a, b):
    return lax.dot_general(a, b, (((1,), (0,)), ((), ())), preferred_element_type=jnp.float32)


def mm_t(a, b):
    return lax.dot_general(a, b, (((1,), (1,)), ((), ())), preferred_element_type=jnp.float32)


def load_rows(ref, plane, first, count):
    return jnp.concatenate(
        [ref[plane, (first + i) * T : (first + i + 1) * T, :] for i in range(count)], axis=1
    )


def store_rows(ref, plane, first, count, value):
    for i in range(count):
        ref[plane, (first + i) * T : (first + i + 1) * T, :] = value[:, i * W : (i + 1) * W]


def get8(ref, plane, first, k):
    return ref[plane, pl.ds(first * T + k, 8, stride=T), :]


def put8(ref, plane, first, k, value):
    ref[plane, pl.ds(first * T + k, 8, stride=T), :] = value


def z_shift(value, step):
    if step == 0:
        return value
    return pltpu.roll(value, step % W, axis=1)


def pad_tile():
    row = lax.broadcasted_iota(jnp.int32, (8, W), 0)
    return jnp.where(row == ONE - 16, 1.0, 0.0).astype(jnp.float32)


def pad_rows(ref, plane, first, count):
    tile = pad_tile()
    for i in range(count):
        ref[plane, (first + i) * T + 16 : (first + i + 1) * T, :] = tile


def chunks(count, size):
    return [(i, min(size, count - i)) for i in range(0, count, size)]


def first_kernel(
    start_hbm, adjoint_hbm, solid_hbm, w_in_t_hbm, b_in_hbm, w_out_hbm, b_out_hbm,
    z, to_even, to_odd, s0, w1x, w2x, w2tx, w1tx, b2b,
    p1, sq, start, adjoint, solid, w_in_t, b_in, w_out, b_out, sems,
):
    pairs = (
        (w_in_t_hbm, w_in_t), (b_in_hbm, b_in), (w_out_hbm, w_out), (b_out_hbm, b_out),
        (start_hbm, start), (solid_hbm, solid), (adjoint_hbm, adjoint),
    )
    copies = [pltpu.make_async_copy(a, b, sems.at[i]) for i, (a, b) in enumerate(pairs)]
    for copy in copies:
        copy.start()
    sq[...] = jnp.zeros((128, 128), jnp.float32)
    for plane in range(2):
        pad_rows(s0, plane, 0, 8)
    for copy in copies[:4]:
        copy.wait()
    sq[0:Q, 0:HID] = w_in_t[...]
    sq[ONE : ONE + 1, 0:HID] = b_in[...]
    a1t = sq[0:T, 0:HID]
    a1 = sq[...].T[0:HID, 0:T]
    sq[...] = jnp.zeros((128, 128), jnp.float32)
    sq[0:Q, 0:HID] = w_out[...]
    a2 = sq[0:T, 0:HID]
    a2t = sq[...].T[0:HID, 0:T]
    sq[...] = jnp.zeros((128, 128), jnp.float32)
    sq[0:1, 0:Q] = b_out[...]
    b2 = jnp.broadcast_to(sq[...].T[0:T, 0:1], (T, W))
    w1 = weights3(a1)
    w2 = weights2(a2)
    w1x[...] = w1
    w2x[...] = w2
    w2tx[...] = weights3(a2t)
    w1tx[...] = weights2(a1t)
    b2b[...] = b2
    w1 = w1.astype(jnp.bfloat16)
    w2 = w2.astype(jnp.bfloat16)
    for copy in copies[4:]:
        copy.wait()
    for plane in range(2):
        for k in range(Q):
            put8(s0, plane, 0, k, start[k, plane])
        sol = solid[plane].astype(jnp.float32)
        z[plane, SOLID] = sol
        mask = sol > 0.5
        for k in range(Q):
            z[plane, Q + place[k]] = jnp.where(
                mask, adjoint[opposite[k], plane], adjoint[k, plane]
            )
    state = jnp.concatenate([load_rows(s0, plane, 0, 8) for plane in range(2)], axis=1)
    hidden = jnp.tanh(mm(w1, stack3(*split(state))))
    change = mm2(w2, split(hidden))
    for i in range(16):
        plane, y = divmod(i, 8)
        fluid = 1.0 - solid[plane, y : y + 1, :].astype(jnp.float32)
        p1[plane, y * T : (y + 1) * T, :] = state[:, i * W : (i + 1) * W] + fluid * (
            change[:, i * W : (i + 1) * W] + b2
        )
    for plane in range(2):
        for k in range(Q):
            z[plane, place[k]] = get8(p1, plane, 0, k)

    def pack(ref, way):
        at = 0
        for plane, unit, rows in y_pieces(way):
            begin = 8 - rows if way == 1 else 0
            ref[at : at + rows, :] = z[plane, unit, begin : begin + rows, :]
            at += rows
        ref[at:, :] = jnp.zeros((Y_ROWS - at, W), jnp.float32)

    odd = lax.rem(lax.axis_index("gy"), 2)

    @pl.when(odd == 0)
    def _():
        pack(to_even, 1)
        pack(to_odd, -1)

    @pl.when(odd == 1)
    def _():
        pack(to_even, -1)
        pack(to_odd, 1)


def near_kernel(z_own, z):
    z[...] = z_own[...]


def second_kernel(z_own, from_even, from_odd, z, to_near, to_far):
    z[:, :, 4:12, :] = z_own[...]

    def unpack(ref, way):
        at = 0
        for plane, unit, rows in y_pieces(way):
            begin = 4 - rows if way == 1 else 12
            z[plane, unit, begin : begin + rows, :] = ref[at : at + rows, :]
            at += rows

    odd = lax.rem(lax.axis_index("gy"), 2)

    @pl.when(odd == 0)
    def _():
        unpack(from_even, -1)
        unpack(from_odd, 1)

    @pl.when(odd == 1)
    def _():
        unpack(from_even, 1)
        unpack(from_odd, -1)

    def pack(ref, way):
        at = 0
        for count, plane, first in far_runs(way):
            ref[at : at + count] = z[plane, first : first + count]
            at += count

    low = lax.rem(lax.axis_index("gx"), 4) < 2

    @pl.when(low)
    def _():
        pack(to_near, 1)
        pack(to_far, -1)

    @pl.when(jnp.logical_not(low))
    def _():
        pack(to_near, -1)
        pack(to_far, 1)


def far_runs(way):
    if way == 1:
        return ((5, 0, 0), (14, 1, 0), (5, 1, Q + 14), (1, 1, SOLID))
    return ((5, 1, 14), (14, 0, 5), (5, 0, Q), (1, 0, SOLID))


FAR = 25


def hold_kernel(f_in, f):
    f[...] = f_in[...]


PLANES = 10
ROWS = 16


def third_kernel(
    scale,
    s0, z_own, z_even, z_odd, f_near, f_far, w1x, w2x, w2tx, w1tx, b2b,
    final_hbm, grad_hbm, sums,
    final, grad, out_sems, zs, s1, p2, s2, p3, gp, g, acc1, acc2, sems,
):
    index = lax.axis_index("gx")
    odd = lax.rem(index, 2)
    high = lax.rem(index, 4) // 2
    copies = [
        (z_even, zs.at[pl.ds(6 - 4 * odd, 2)]),
        (z_own, zs.at[4:6]),
        (z_odd, zs.at[pl.ds(2 + 4 * odd, 2)]),
    ]
    for ref, left in ((f_near, high), (f_far, 1 - high)):
        at = 0
        for (count, plane, first), (_, plane_r, first_r) in zip(far_runs(1), far_runs(-1)):
            plane_r += 8
            x = plane_r + left * (plane - plane_r)
            unit = first_r + left * (first - first_r)
            copies.append((ref.at[at : at + count], zs.at[x, pl.ds(unit, count)]))
            at += count
    copies = [pltpu.make_async_copy(a, b, sems.at[i]) for i, (a, b) in enumerate(copies)]
    for copy in copies:
        copy.start()

    w1 = w1x[...].astype(jnp.bfloat16)
    w2 = w2x[...].astype(jnp.bfloat16)
    w2t = w2tx[...].astype(jnp.bfloat16)
    w1t = w1tx[...].astype(jnp.bfloat16)
    b2 = b2b[...]
    acc1[...] = jnp.zeros(acc1.shape, jnp.float32)
    acc2[...] = jnp.zeros(acc2.shape, jnp.float32)
    for ref, planes in ((s1, 8), (s2, 6)):
        for plane in range(planes):
            pad_rows(ref, plane, 0, ROWS)
    for plane in range(6):
        for i in range(ROWS):
            gp[plane, i * T + 16 : (i + 1) * T, :] = jnp.zeros((8, W), jnp.float32)

    for copy in copies:
        copy.wait()

    def fluid_rows(x, y):
        return 1.0 - zs[x, SOLID, y : y + 1, :]

    def forward_hidden(state_parts):
        return jnp.tanh(mm(w1, stack3(*state_parts)))

    def collide(p_ref, p_plane, zx, first, count, state, hidden_parts):
        change = mm2(w2, hidden_parts)
        for i in range(count):
            y = first + i
            p_ref[p_plane, y * T : (y + 1) * T, :] = state[:, i * W : (i + 1) * W] + fluid_rows(
                zx, y
            ) * (change[:, i * W : (i + 1) * W] + b2)

    def backward(own, zx, first, count, state_parts, hidden, hidden_parts, grad_post):
        change = jnp.concatenate(
            [
                fluid_rows(zx, first + i) * grad_post[:, i * W : (i + 1) * W]
                for i in range(count)
            ],
            axis=1,
        )
        change_parts = split(change)
        grad_hidden = mm(w2t, stack3(*change_parts))
        grad_pre = grad_hidden * (1.0 - hidden * hidden)
        pre_parts = split(grad_pre)
        back = grad_post + mm2(w1t, pre_parts)
        low = max(first, 4)
        high = min(first + count, 12)

        if own and high > low:
            part = slice((low - first) * W, (high - first) * W)
            left = jnp.concatenate([a[:, part] for a in state_parts], axis=0)
            right = jnp.concatenate([a[:, part] for a in pre_parts + change_parts], axis=0)
            acc1[...] += mm_t(left.astype(jnp.bfloat16), right.astype(jnp.bfloat16))
            left = jnp.concatenate([a[:, part] for a in change_parts], axis=0)
            right = jnp.concatenate([a[:, part] for a in hidden_parts], axis=0)
            acc2[...] += mm_t(left.astype(jnp.bfloat16), right.astype(jnp.bfloat16))
        return back

    def over_planes(halo, body):
        if halo:
            lax.fori_loop(
                0,
                2 * halo,
                lambda i, c: body(False, jnp.where(i < halo, i, i + 2), c),
                0,
                unroll=2 * halo,
            )
        lax.fori_loop(0, 2, lambda i, c: body(True, i + halo, c), 0, unroll=2)

    def reflect(values, mask):
        return [jnp.where(mask, values[opposite[k]], values[k]) for k in range(Q)]

    def stage1(j, carry):
        zx = j + 1
        for y in (1, 7):
            moved = []
            for k in range(Q):
                cx, cy, cz = velocities[k]
                moved.append(z_shift(zs[zx - cx, place[k], y - cy : y - cy + 8, :], cz))
            moved = reflect(moved, zs[zx, SOLID, y : y + 8, :] > 0.5)
            for k in range(Q):
                put8(s1, j, y, k, moved[k])
        for first, count in chunks(14, 14):
            first += 1
            state = load_rows(s1, j, first, count)
            hidden = forward_hidden(split(state))
            collide(p2, j, zx, first, count, state, split(hidden))
        return carry

    lax.fori_loop(0, 8, stage1, 0, unroll=8)

    def stage2(own, j, carry):
        zx = j + 2
        for y in (2, 6):
            moved = []
            for k in range(Q):
                cx, cy, cz = velocities[k]
                moved.append(z_shift(get8(p2, j + 1 - cx, y - cy, k), cz))
            moved = reflect(moved, zs[zx, SOLID, y : y + 8, :] > 0.5)
            for k in range(Q):
                put8(s2, j, y, k, moved[k])
            for k in range(Q):
                cx, cy, cz = velocities[k]
                value = zs[zx + cx, Q + place[k], y + cy : y + cy + 8, :]
                put8(gp, j, y, k, z_shift(value, -cz))
        for first, count in chunks(12, 12):
            first += 2
            state = load_rows(s2, j, first, count)
            state_parts = split(state)
            hidden = forward_hidden(state_parts)
            hidden_parts = split(hidden)
            collide(p3, j, zx, first, count, state, hidden_parts)
            grad_post = load_rows(gp, j, first, count)
            back = backward(own, zx, first, count, state_parts, hidden, hidden_parts, grad_post)
            store_rows(g, j, first, count, back)
        return carry

    over_planes(2, stage2)

    for plane in range(2):
        moved = []
        for k in range(Q):
            cx, cy, cz = velocities[k]
            moved.append(z_shift(get8(p3, plane + 2 - cx, 4 - cy, k), cz))
        moved = reflect(moved, zs[plane + 4, SOLID, 4:12, :] > 0.5)
        for k in range(Q):
            final[k, plane] = moved[k]
    final_copy = pltpu.make_async_copy(final, final_hbm, out_sems.at[0])
    final_copy.start()

    def run_back(g_ref, g_plane, zx, y, out_plane):
        for k in range(Q):
            cx, cy, cz = velocities[k]
            one = get8(g_ref, g_plane + cx, y + cy, k)
            if k != 0:
                other = get8(g_ref, g_plane + cx, y + cy, opposite[k])
                mask = zs[zx + cx, SOLID, y + cy : y + cy + 8, :] > 0.5
                one = jnp.where(mask, other, one)
            put8(gp, out_plane, y, k, z_shift(one, -cz))

    def stage3(own, j, carry):
        zx = j + 3
        for y in (3, 5):
            run_back(g, j + 1, zx, y, j)
        for first, count in ((3, 10),):
            state_parts = split(load_rows(s1, j + 2, first, count))
            hidden = forward_hidden(state_parts)
            grad_post = load_rows(gp, j, first, count)
            back = backward(own, zx, first, count, state_parts, hidden, split(hidden), grad_post)
            store_rows(p2, j, first, count, back)
        return carry

    over_planes(1, stage3)

    def stage4(own, j, carry):
        zx = j + 4
        run_back(p2, j + 1, zx, 4, j)
        for first, count in ((4, 8),):
            state_parts = split(load_rows(s0, j, first - 4, count))
            hidden = forward_hidden(state_parts)
            grad_post = load_rows(gp, j, first, count)
            back = backward(own, zx, first, count, state_parts, hidden, split(hidden), grad_post)
            store_rows(g, j, first, count, back)
        for k in range(Q):
            grad[k, j] = get8(g, j, 4, k)
        return carry

    over_planes(0, stage4)
    grad_copy = pltpu.make_async_copy(grad, grad_hbm, out_sems.at[1])
    grad_copy.start()

    one = acc1[0:T, :] + acc1[T : 2 * T, :]
    two = acc2[0:T, :] + acc2[T : 2 * T, :]
    in_part = one[:, 0:HID] + one[:, HID : 2 * HID]
    out_part = two[:, 0:HID] + two[:, HID : 2 * HID]
    bias = one[:, 2 * HID : 2 * HID + T] + one[:, 2 * HID + T : 2 * HID + 2 * T]
    sums[...] = jnp.zeros(sums.shape, jnp.float32)
    sums[0:T, 0:HID] = in_part * scale
    sums[0:Q, HID : 2 * HID] = out_part[0:Q, :] * scale
    sums[ONE : ONE + 1, HID : HID + T] = bias[ONE : ONE + 1, :] * scale
    final_copy.wait()
    grad_copy.wait()


def last_kernel(parts, grad_w_in_t, grad_b_in, grad_w_out, grad_b_out):
    total = parts[0]
    for i in range(1, parts.shape[0]):
        total = total + parts[i]
    grad_w_in_t[...] = total[0:Q, 0:HID]
    grad_b_in[...] = total[ONE : ONE + 1, 0:HID]
    grad_w_out[...] = total[0:Q, HID : 2 * HID]
    grad_b_out[...] = total[ONE : ONE + 1, HID : HID + Q]


def swap_even(x, axis, step=1):
    count = lax.axis_size(axis)
    return lax.ppermute(x, axis, [(i, i ^ step) for i in range(count)])


def swap_odd(x, axis, step=1):
    count = lax.axis_size(axis)
    return lax.ppermute(
        x, axis, [(i, (i + step if i & step else i - step) % count) for i in range(count)]
    )


def spread(x, groups):
    count = len(groups[0])
    return lax.all_to_all(
        jnp.broadcast_to(x[None], (count,) + x.shape), ("gx", "gy"), 0, 0, axis_index_groups=groups
    )


def sum_groups():
    gx, gy = lax.axis_size("gx"), lax.axis_size("gy")
    nx, ny = math.gcd(gx, 8), math.gcd(gy, 8)
    zs = [(a, b) for b in range(gy // ny) for a in range(gx // nx)]

    def at(z, x, y):
        return (z[0] * nx + x) * gy + z[1] * ny + y

    return (
        [[at(z, x, y) for x in range(nx)] for z in zs for y in range(ny)],
        [[at(z, x, y) for z in zs] for x in range(nx) for y in range(ny)],
        [[at(z, x, y) for y in range(ny)] for z in zs for x in range(nx)],
    )


F32 = jnp.float32


def shape(*dims):
    return jax.ShapeDtypeStruct(dims, F32)


FIRST_VMEM = 63 * 1024 * 1024
PARAMS = pltpu.CompilerParams(vmem_limit_bytes=48 * 1024 * 1024)


def on_device(start, adjoint, solid, w_in, b_in, w_out, b_out):
    rows = pltpu.VMEM
    z, to_even, to_odd, s0, w1x, w2x, w2tx, w1tx, b2b = pl.pallas_call(
        first_kernel,
        out_shape=(
            shape(2, UNITS, 8, W),
            shape(Y_ROWS, W),
            shape(Y_ROWS, W),
            shape(2, 8 * T, W),
            shape(HID, 80),
            shape(2 * T, 2 * HID),
            shape(HID, 80),
            shape(2 * T, 2 * HID),
            shape(T, W),
        ),
        in_specs=[pl.BlockSpec(memory_space=pltpu.HBM)] * 7,
        scratch_shapes=[
            rows((2, 8 * T, W), F32),
            rows((128, 128), F32),
            rows((Q, 2, 8, W), F32),
            rows((Q, 2, 8, W), F32),
            rows((2, 8, W), jnp.int32),
            rows((Q, HID), F32),
            rows((1, HID), F32),
            rows((Q, HID), F32),
            rows((1, Q), F32),
            pltpu.SemaphoreType.DMA((7,)),
        ],
        compiler_params=pltpu.CompilerParams(vmem_limit_bytes=FIRST_VMEM),
        name="first",
    )(start, adjoint, solid, w_in.T, b_in.reshape(1, HID), w_out, b_out.reshape(1, Q))

    from_even = swap_even(to_even, "gy")
    from_odd = swap_odd(to_odd, "gy")

    z = pl.pallas_call(
        near_kernel,
        out_shape=shape(2, UNITS, 8, W),
        compiler_params=PARAMS,
        name="near",
    )(z)
    z, to_near, to_far = pl.pallas_call(
        second_kernel,
        out_shape=(shape(2, UNITS, ROWS, W), shape(FAR, ROWS, W), shape(FAR, ROWS, W)),
        compiler_params=PARAMS,
        name="second",
    )(z, from_even, from_odd)

    z_odd = swap_odd(z, "gx")
    f_far = swap_odd(to_far, "gx", 2)
    f_near = swap_even(to_near, "gx", 2)
    z_even = swap_even(z, "gx")

    f_far = pl.pallas_call(
        hold_kernel,
        out_shape=shape(FAR, ROWS, W),
        compiler_params=PARAMS,
        cost_estimate=pl.CostEstimate(flops=6 * 10**9, bytes_accessed=10**6, transcendentals=0),
        name="hold",
    )(f_far)

    cells = 16 * W * lax.axis_size("gx") * lax.axis_size("gy")
    vmem = pl.BlockSpec(memory_space=pltpu.VMEM)
    hbm = pl.BlockSpec(memory_space=pl.ANY)
    final, grad, sums = pl.pallas_call(
        functools.partial(third_kernel, 1.0 / math.sqrt(cells)),
        out_shape=(shape(Q, 2, 8, W), shape(Q, 2, 8, W), shape(T, W)),
        in_specs=[vmem] + [hbm] * 5 + [vmem] * 5,
        out_specs=(hbm, hbm, vmem),
        scratch_shapes=[
            rows((Q, 2, 8, W), F32),
            rows((Q, 2, 8, W), F32),
            pltpu.SemaphoreType.DMA((2,)),
            rows((PLANES, UNITS, ROWS, W), F32),
            rows((8, ROWS * T, W), F32),
            rows((8, ROWS * T, W), F32),
            rows((6, ROWS * T, W), F32),
            rows((6, ROWS * T, W), F32),
            rows((6, ROWS * T, W), F32),
            rows((6, ROWS * T, W), F32),
            rows((2 * T, 2 * HID + 2 * T), F32),
            rows((2 * T, 2 * HID), F32),
            pltpu.SemaphoreType.DMA((11,)),
        ],
        compiler_params=PARAMS,
        name="third",
    )(s0, z, z_even, z_odd, f_near, f_far, w1x, w2x, w2tx, w1tx, b2b)

    along_x, along_z, along_y = sum_groups()
    sums = spread(sums, along_x).sum(0)
    sums = spread(sums, along_z).sum(0)
    grad_w_in_t, grad_b_in, grad_w_out, grad_b_out = pl.pallas_call(
        last_kernel,
        out_shape=(shape(Q, HID), shape(1, HID), shape(Q, HID), shape(1, Q)),
        compiler_params=PARAMS,
        name="last",
    )(spread(sums, along_y))
    return final, grad, grad_w_in_t.T, grad_b_in[0], grad_w_out, grad_b_out[0]


def solution(mesh):
    return jax.shard_map(
        on_device,
        mesh=mesh,
        in_specs=(
            P(None, "gx", "gy", None),
            P(None, "gx", "gy", None),
            P("gx", "gy", None),
            P(),
            P(),
            P(),
            P(),
        ),
        out_specs=(P(None, "gx", "gy", None), P(None, "gx", "gy", None), P(), P(), P(), P()),
        check_vma=False,
    )
```

```python
import functools
import math

import jax
import jax.numpy as jnp
from jax import lax
from jax.experimental import pallas as pl
from jax.experimental.pallas import tpu as pltpu
from jax.sharding import PartitionSpec as P

Q = 19
HID = 64
T = 24
ONE = 19
W = 128

velocities = (
    (0, 0, 0),
    (1, 0, 0),
    (-1, 0, 0),
    (0, 1, 0),
    (0, -1, 0),
    (0, 0, 1),
    (0, 0, -1),
    (1, 1, 0),
    (-1, -1, 0),
    (1, -1, 0),
    (-1, 1, 0),
    (1, 0, 1),
    (-1, 0, -1),
    (1, 0, -1),
    (-1, 0, 1),
    (0, 1, 1),
    (0, -1, -1),
    (0, 1, -1),
    (0, -1, 1),
)
opposite = (0, 2, 1, 4, 3, 6, 5, 8, 7, 10, 9, 12, 11, 14, 13, 16, 15, 18, 17)

order = tuple(sorted(range(Q), key=lambda k: -velocities[k][0]))
place = {k: i for i, k in enumerate(order)}
UNITS = 2 * Q + 1
SOLID = 2 * Q


def y_pieces(way):
    pieces = []
    for plane in range(2):
        for k in range(Q):
            pieces.append((plane, place[k], 3 + way * velocities[k][1]))
        for k in range(Q):
            pieces.append((plane, Q + place[k], 2 - way * velocities[k][1]))
        pieces.append((plane, SOLID, 3))
    return pieces


Y_ROWS = 200


def split(a):
    high = a.astype(jnp.bfloat16).astype(jnp.float32)
    return high, a - high


def stack3(high, low):
    parts = [high, low, high]
    if (3 * high.shape[0]) % 16:
        parts.append(jnp.zeros((8, high.shape[1]), jnp.float32))
    return jnp.concatenate(parts, axis=0).astype(jnp.bfloat16)


def weights3(a):
    high, low = split(a)
    parts = [high, high, low]
    if (3 * a.shape[1]) % 16:
        parts.append(jnp.zeros((a.shape[0], 8), jnp.float32))
    return jnp.concatenate(parts, axis=1)


def weights2(a):
    high, low = split(a)
    top = jnp.concatenate([high, high], axis=1)
    bottom = jnp.concatenate([low, jnp.zeros_like(low)], axis=1)
    return jnp.concatenate([top, bottom], axis=0)


def mm2(weights, parts):
    both = mm(weights, jnp.concatenate(parts, axis=0).astype(jnp.bfloat16))
    return both[0:T] + both[T:]


def mm(a, b):
    return lax.dot_general(a, b, (((1,), (0,)), ((), ())), preferred_element_type=jnp.float32)


def mm_t(a, b):
    return lax.dot_general(a, b, (((1,), (1,)), ((), ())), preferred_element_type=jnp.float32)


def load_rows(ref, plane, first, count):
    return jnp.concatenate(
        [ref[plane, (first + i) * T : (first + i + 1) * T, :] for i in range(count)], axis=1
    )


def store_rows(ref, plane, first, count, value):
    for i in range(count):
        ref[plane, (first + i) * T : (first + i + 1) * T, :] = value[:, i * W : (i + 1) * W]


def get8(ref, plane, first, k):
    return ref[plane, pl.ds(first * T + k, 8, stride=T), :]


def put8(ref, plane, first, k, value):
    ref[plane, pl.ds(first * T + k, 8, stride=T), :] = value


def z_shift(value, step):
    if step == 0:
        return value
    return pltpu.roll(value, step % W, axis=1)


def pad_tile():
    row = lax.broadcasted_iota(jnp.int32, (8, W), 0)
    return jnp.where(row == ONE - 16, 1.0, 0.0).astype(jnp.float32)


def pad_rows(ref, plane, first, count):
    tile = pad_tile()
    for i in range(count):
        ref[plane, (first + i) * T + 16 : (first + i + 1) * T, :] = tile


def reflect(values, mask):
    return [jnp.where(mask, values[opposite[k]], values[k]) for k in range(Q)]


def chunks(count, size):
    return [(i, min(size, count - i)) for i in range(0, count, size)]


def first_kernel(
    start_hbm, adjoint_hbm, solid_hbm, w_in_t_hbm, b_in_hbm, w_out_hbm, b_out_hbm,
    z, to_even, to_odd, s0, w1x, w2x, w2tx, w1tx, b2b,
    p1, sq, start, adjoint, solid, w_in_t, b_in, w_out, b_out, sems,
):
    pairs = (
        (w_in_t_hbm, w_in_t), (b_in_hbm, b_in), (w_out_hbm, w_out), (b_out_hbm, b_out),
        (start_hbm, start), (solid_hbm, solid), (adjoint_hbm, adjoint),
    )
    copies = [pltpu.make_async_copy(a, b, sems.at[i]) for i, (a, b) in enumerate(pairs)]
    for copy in copies:
        copy.start()
    sq[...] = jnp.zeros((128, 128), jnp.float32)
    for plane in range(2):
        pad_rows(s0, plane, 0, 8)
    for copy in copies[:4]:
        copy.wait()
    sq[0:Q, 0:HID] = w_in_t[...]
    sq[ONE : ONE + 1, 0:HID] = b_in[...]
    a1t = sq[0:T, 0:HID]
    a1 = sq[...].T[0:HID, 0:T]
    sq[...] = jnp.zeros((128, 128), jnp.float32)
    sq[0:Q, 0:HID] = w_out[...]
    a2 = sq[0:T, 0:HID]
    a2t = sq[...].T[0:HID, 0:T]
    sq[...] = jnp.zeros((128, 128), jnp.float32)
    sq[0:1, 0:Q] = b_out[...]
    b2 = jnp.broadcast_to(sq[...].T[0:T, 0:1], (T, W))
    w1 = weights3(a1)
    w2 = weights2(a2)
    w1x[...] = w1
    w2x[...] = w2
    w2tx[...] = weights3(a2t)
    w1tx[...] = weights2(a1t)
    b2b[...] = b2
    w1 = w1.astype(jnp.bfloat16)
    w2 = w2.astype(jnp.bfloat16)
    for copy in copies[4:]:
        copy.wait()
    for plane in range(2):
        for k in range(Q):
            put8(s0, plane, 0, k, start[k, plane])
        sol = solid[plane].astype(jnp.float32)
        z[plane, SOLID] = sol
        mask = sol > 0.5
        for k in range(Q):
            z[plane, Q + place[k]] = jnp.where(
                mask, adjoint[opposite[k], plane], adjoint[k, plane]
            )
    state = jnp.concatenate([load_rows(s0, plane, 0, 8) for plane in range(2)], axis=1)
    hidden = jnp.tanh(mm(w1, stack3(*split(state))))
    change = mm2(w2, split(hidden))
    for i in range(16):
        plane, y = divmod(i, 8)
        fluid = 1.0 - solid[plane, y : y + 1, :].astype(jnp.float32)
        p1[plane, y * T : (y + 1) * T, :] = state[:, i * W : (i + 1) * W] + fluid * (
            change[:, i * W : (i + 1) * W] + b2
        )
    for plane in range(2):
        for k in range(Q):
            z[plane, place[k]] = get8(p1, plane, 0, k)

    def pack(ref, way):
        at = 0
        for plane, unit, rows in y_pieces(way):
            begin = 8 - rows if way == 1 else 0
            ref[at : at + rows, :] = z[plane, unit, begin : begin + rows, :]
            at += rows
        ref[at:, :] = jnp.zeros((Y_ROWS - at, W), jnp.float32)

    odd = lax.rem(lax.axis_index("gy"), 2)

    @pl.when(odd == 0)
    def _():
        pack(to_even, 1)
        pack(to_odd, -1)

    @pl.when(odd == 1)
    def _():
        pack(to_even, -1)
        pack(to_odd, 1)


def near_kernel(z_own, z):
    z[...] = z_own[...]


def second_kernel(z_own, from_even, from_odd, z, to_near, to_far):
    z[:, :, 4:12, :] = z_own[...]

    def unpack(ref, way):
        at = 0
        for plane, unit, rows in y_pieces(way):
            begin = 4 - rows if way == 1 else 12
            z[plane, unit, begin : begin + rows, :] = ref[at : at + rows, :]
            at += rows

    odd = lax.rem(lax.axis_index("gy"), 2)

    @pl.when(odd == 0)
    def _():
        unpack(from_even, -1)
        unpack(from_odd, 1)

    @pl.when(odd == 1)
    def _():
        unpack(from_even, 1)
        unpack(from_odd, -1)

    def pack(ref, way):
        at = 0
        for count, plane, first in far_runs(way):
            ref[at : at + count] = z[plane, first : first + count]
            at += count

    low = lax.rem(lax.axis_index("gx"), 4) < 2

    @pl.when(low)
    def _():
        pack(to_near, 1)
        pack(to_far, -1)

    @pl.when(jnp.logical_not(low))
    def _():
        pack(to_near, -1)
        pack(to_far, 1)


def far_runs(way):
    if way == 1:
        return ((5, 0, 0), (14, 1, 0), (5, 1, Q + 14), (1, 1, SOLID))
    return ((5, 1, 14), (14, 0, 5), (5, 0, Q), (1, 0, SOLID))


FAR = 25


def hold_kernel(f_in, f):
    f[...] = f_in[...]


PLANES = 10
ROWS = 16


def third_kernel(
    scale,
    s0, z_own, z_even, z_odd, f_near, f_far, w1x, w2x, w2tx, w1tx, b2b,
    sums, p3, g,
    zs, s1, p2, s2, gp, acc1, acc2, sems,
):
    index = lax.axis_index("gx")
    odd = lax.rem(index, 2)
    high = lax.rem(index, 4) // 2
    copies = [
        (z_even, zs.at[pl.ds(6 - 4 * odd, 2)]),
        (z_own, zs.at[4:6]),
        (z_odd, zs.at[pl.ds(2 + 4 * odd, 2)]),
    ]
    for ref, left in ((f_near, high), (f_far, 1 - high)):
        at = 0
        for (count, plane, first), (_, plane_r, first_r) in zip(far_runs(1), far_runs(-1)):
            plane_r += 8
            x = plane_r + left * (plane - plane_r)
            unit = first_r + left * (first - first_r)
            copies.append((ref.at[at : at + count], zs.at[x, pl.ds(unit, count)]))
            at += count
    copies = [pltpu.make_async_copy(a, b, sems.at[i]) for i, (a, b) in enumerate(copies)]
    for copy in copies:
        copy.start()

    w1 = w1x[...].astype(jnp.bfloat16)
    w2 = w2x[...].astype(jnp.bfloat16)
    w2t = w2tx[...].astype(jnp.bfloat16)
    w1t = w1tx[...].astype(jnp.bfloat16)
    b2 = b2b[...]
    acc1[...] = jnp.zeros(acc1.shape, jnp.float32)
    acc2[...] = jnp.zeros(acc2.shape, jnp.float32)
    for ref, planes in ((s1, 8), (s2, 6)):
        for plane in range(planes):
            pad_rows(ref, plane, 0, ROWS)
    for plane in range(6):
        for i in range(ROWS):
            gp[plane, i * T + 16 : (i + 1) * T, :] = jnp.zeros((8, W), jnp.float32)

    for copy in copies[:3]:
        copy.wait()

    def fluid_rows(x, y):
        return 1.0 - zs[x, SOLID, y : y + 1, :]

    def forward_hidden(state_parts):
        return jnp.tanh(mm(w1, stack3(*state_parts)))

    def collide(p_ref, p_plane, zx, first, count, state, hidden_parts):
        change = mm2(w2, hidden_parts)
        for i in range(count):
            y = first + i
            p_ref[p_plane, y * T : (y + 1) * T, :] = state[:, i * W : (i + 1) * W] + fluid_rows(
                zx, y
            ) * (change[:, i * W : (i + 1) * W] + b2)

    def backward(own, zx, first, count, state_parts, hidden, hidden_parts, grad_post):
        change = jnp.concatenate(
            [
                fluid_rows(zx, first + i) * grad_post[:, i * W : (i + 1) * W]
                for i in range(count)
            ],
            axis=1,
        )
        change_parts = split(change)
        grad_hidden = mm(w2t, stack3(*change_parts))
        grad_pre = grad_hidden * (1.0 - hidden * hidden)
        pre_parts = split(grad_pre)
        back = grad_post + mm2(w1t, pre_parts)
        low = max(first, 4)
        high = min(first + count, 12)

        if own and high > low:
            part = slice((low - first) * W, (high - first) * W)
            left = jnp.concatenate([a[:, part] for a in state_parts], axis=0)
            right = jnp.concatenate([a[:, part] for a in pre_parts + change_parts], axis=0)
            acc1[...] += mm_t(left.astype(jnp.bfloat16), right.astype(jnp.bfloat16))
            left = jnp.concatenate([a[:, part] for a in change_parts], axis=0)
            right = jnp.concatenate([a[:, part] for a in hidden_parts], axis=0)
            acc2[...] += mm_t(left.astype(jnp.bfloat16), right.astype(jnp.bfloat16))
        return back

    def over_planes(halo, body):
        if halo:
            lax.fori_loop(
                0,
                2 * halo,
                lambda i, c: body(False, jnp.where(i < halo, i, i + 2), c),
                0,
                unroll=2 * halo,
            )
        lax.fori_loop(0, 2, lambda i, c: body(True, i + halo, c), 0, unroll=2)

    def stage1(j, carry):
        zx = j + 1
        for y in (1, 7):
            moved = []
            for k in range(Q):
                cx, cy, cz = velocities[k]
                moved.append(z_shift(zs[zx - cx, place[k], y - cy : y - cy + 8, :], cz))
            moved = reflect(moved, zs[zx, SOLID, y : y + 8, :] > 0.5)
            for k in range(Q):
                put8(s1, j, y, k, moved[k])
        for first, count in chunks(14, 14):
            first += 1
            state = load_rows(s1, j, first, count)
            hidden = forward_hidden(split(state))
            collide(p2, j, zx, first, count, state, split(hidden))
        return carry

    lax.fori_loop(2, 6, stage1, 0, unroll=4)
    for copy in copies[3:]:
        copy.wait()
    lax.fori_loop(0, 4, lambda i, c: stage1(jnp.where(i < 2, i, i + 4), c), 0, unroll=4)

    def stage2(own, j, carry):
        zx = j + 2
        for y in (2, 6):
            moved = []
            for k in range(Q):
                cx, cy, cz = velocities[k]
                moved.append(z_shift(get8(p2, j + 1 - cx, y - cy, k), cz))
            moved = reflect(moved, zs[zx, SOLID, y : y + 8, :] > 0.5)
            for k in range(Q):
                put8(s2, j, y, k, moved[k])
            for k in range(Q):
                cx, cy, cz = velocities[k]
                value = zs[zx + cx, Q + place[k], y + cy : y + cy + 8, :]
                put8(gp, j, y, k, z_shift(value, -cz))
        for first, count in chunks(12, 12):
            first += 2
            state = load_rows(s2, j, first, count)
            state_parts = split(state)
            hidden = forward_hidden(state_parts)
            hidden_parts = split(hidden)
            collide(p3, j, zx, first, count, state, hidden_parts)
            grad_post = load_rows(gp, j, first, count)
            back = backward(own, zx, first, count, state_parts, hidden, hidden_parts, grad_post)
            store_rows(g, j, first, count, back)
        return carry

    over_planes(2, stage2)

    def run_back(g_ref, g_plane, zx, y, out_plane):
        for k in range(Q):
            cx, cy, cz = velocities[k]
            one = get8(g_ref, g_plane + cx, y + cy, k)
            if k != 0:
                other = get8(g_ref, g_plane + cx, y + cy, opposite[k])
                mask = zs[zx + cx, SOLID, y + cy : y + cy + 8, :] > 0.5
                one = jnp.where(mask, other, one)
            put8(gp, out_plane, y, k, z_shift(one, -cz))

    def stage3(own, j, carry):
        zx = j + 3
        for y in (3, 5):
            run_back(g, j + 1, zx, y, j)
        for first, count in ((3, 10),):
            state_parts = split(load_rows(s1, j + 2, first, count))
            hidden = forward_hidden(state_parts)
            grad_post = load_rows(gp, j, first, count)
            back = backward(own, zx, first, count, state_parts, hidden, split(hidden), grad_post)
            store_rows(p2, j, first, count, back)
        return carry

    over_planes(1, stage3)

    def stage4(own, j, carry):
        zx = j + 4
        run_back(p2, j + 1, zx, 4, j)
        for first, count in ((4, 8),):
            state_parts = split(load_rows(s0, j, first - 4, count))
            hidden = forward_hidden(state_parts)
            grad_post = load_rows(gp, j, first, count)
            back = backward(own, zx, first, count, state_parts, hidden, split(hidden), grad_post)
            store_rows(g, j, first, count, back)
        return carry

    over_planes(0, stage4)

    one = acc1[0:T, :] + acc1[T : 2 * T, :]
    two = acc2[0:T, :] + acc2[T : 2 * T, :]
    in_part = one[:, 0:HID] + one[:, HID : 2 * HID]
    out_part = two[:, 0:HID] + two[:, HID : 2 * HID]
    bias = one[:, 2 * HID : 2 * HID + T] + one[:, 2 * HID + T : 2 * HID + 2 * T]
    sums[...] = jnp.zeros(sums.shape, jnp.float32)
    sums[0:T, 0:HID] = in_part * scale
    sums[0:Q, HID : 2 * HID] = out_part[0:Q, :] * scale
    sums[ONE : ONE + 1, HID : HID + T] = bias[ONE : ONE + 1, :] * scale


def fourth_kernel(z, p3, g, final, grad):
    for plane in range(2):
        moved = []
        for k in range(Q):
            cx, cy, cz = velocities[k]
            moved.append(z_shift(get8(p3, plane + 2 - cx, 4 - cy, k), cz))
        moved = reflect(moved, z[plane, SOLID, 4:12, :] > 0.5)
        for k in range(Q):
            final[k, plane] = moved[k]
            grad[k, plane] = get8(g, plane, 4, k)


def last_kernel(parts, grad_w_in_t, grad_b_in, grad_w_out, grad_b_out):
    total = parts[0]
    for i in range(1, parts.shape[0]):
        total = total + parts[i]
    grad_w_in_t[...] = total[0:Q, 0:HID]
    grad_b_in[...] = total[ONE : ONE + 1, 0:HID]
    grad_w_out[...] = total[0:Q, HID : 2 * HID]
    grad_b_out[...] = total[ONE : ONE + 1, HID : HID + Q]


def swap_even(x, axis, step=1):
    count = lax.axis_size(axis)
    return lax.ppermute(x, axis, [(i, i ^ step) for i in range(count)])


def swap_odd(x, axis, step=1):
    count = lax.axis_size(axis)
    return lax.ppermute(
        x, axis, [(i, (i + step if i & step else i - step) % count) for i in range(count)]
    )


def spread(x, groups):
    count = len(groups[0])
    return lax.all_to_all(
        jnp.broadcast_to(x[None], (count,) + x.shape), ("gx", "gy"), 0, 0, axis_index_groups=groups
    )


def sum_groups():
    gx, gy = lax.axis_size("gx"), lax.axis_size("gy")
    nx, ny = math.gcd(gx, 8), math.gcd(gy, 8)
    zs = [(a, b) for b in range(gy // ny) for a in range(gx // nx)]

    def at(z, x, y):
        return (z[0] * nx + x) * gy + z[1] * ny + y

    return (
        [[at(z, x, y) for x in range(nx)] for z in zs for y in range(ny)],
        [[at(z, x, y) for z in zs] for x in range(nx) for y in range(ny)],
        [[at(z, x, y) for y in range(ny)] for z in zs for x in range(nx)],
    )


F32 = jnp.float32


def shape(*dims):
    return jax.ShapeDtypeStruct(dims, F32)


FIRST_VMEM = 63 * 1024 * 1024
PARAMS = pltpu.CompilerParams(vmem_limit_bytes=48 * 1024 * 1024)


def on_device(start, adjoint, solid, w_in, b_in, w_out, b_out):
    rows = pltpu.VMEM
    z, to_even, to_odd, s0, w1x, w2x, w2tx, w1tx, b2b = pl.pallas_call(
        first_kernel,
        out_shape=(
            shape(2, UNITS, 8, W),
            shape(Y_ROWS, W),
            shape(Y_ROWS, W),
            shape(2, 8 * T, W),
            shape(HID, 80),
            shape(2 * T, 2 * HID),
            shape(HID, 80),
            shape(2 * T, 2 * HID),
            shape(T, W),
        ),
        in_specs=[pl.BlockSpec(memory_space=pltpu.HBM)] * 7,
        scratch_shapes=[
            rows((2, 8 * T, W), F32),
            rows((128, 128), F32),
            rows((Q, 2, 8, W), F32),
            rows((Q, 2, 8, W), F32),
            rows((2, 8, W), jnp.int32),
            rows((Q, HID), F32),
            rows((1, HID), F32),
            rows((Q, HID), F32),
            rows((1, Q), F32),
            pltpu.SemaphoreType.DMA((7,)),
        ],
        compiler_params=pltpu.CompilerParams(vmem_limit_bytes=FIRST_VMEM),
        name="first",
    )(start, adjoint, solid, w_in.T, b_in.reshape(1, HID), w_out, b_out.reshape(1, Q))

    from_even = swap_even(to_even, "gy")
    from_odd = swap_odd(to_odd, "gy")

    z = pl.pallas_call(
        near_kernel,
        out_shape=shape(2, UNITS, 8, W),
        compiler_params=PARAMS,
        name="near",
    )(z)
    z, to_near, to_far = pl.pallas_call(
        second_kernel,
        out_shape=(shape(2, UNITS, ROWS, W), shape(FAR, ROWS, W), shape(FAR, ROWS, W)),
        compiler_params=PARAMS,
        name="second",
    )(z, from_even, from_odd)

    z_odd = swap_odd(z, "gx")
    f_far = swap_odd(to_far, "gx", 2)
    f_near = swap_even(to_near, "gx", 2)
    z_even = swap_even(z, "gx")

    f_far = pl.pallas_call(
        hold_kernel,
        out_shape=shape(FAR, ROWS, W),
        compiler_params=PARAMS,
        cost_estimate=pl.CostEstimate(flops=6 * 10**9, bytes_accessed=10**6, transcendentals=0),
        name="hold",
    )(f_far)

    cells = 16 * W * lax.axis_size("gx") * lax.axis_size("gy")
    vmem = pl.BlockSpec(memory_space=pltpu.VMEM)
    hbm = pl.BlockSpec(memory_space=pl.ANY)
    sums, p3, g = pl.pallas_call(
        functools.partial(third_kernel, 1.0 / math.sqrt(cells)),
        out_shape=(shape(T, W), shape(6, ROWS * T, W), shape(6, ROWS * T, W)),
        in_specs=[vmem] + [hbm] * 5 + [vmem] * 5,
        out_specs=(vmem, vmem, vmem),
        scratch_shapes=[
            rows((PLANES, UNITS, ROWS, W), F32),
            rows((8, ROWS * T, W), F32),
            rows((8, ROWS * T, W), F32),
            rows((6, ROWS * T, W), F32),
            rows((6, ROWS * T, W), F32),
            rows((2 * T, 2 * HID + 2 * T), F32),
            rows((2 * T, 2 * HID), F32),
            pltpu.SemaphoreType.DMA((11,)),
        ],
        compiler_params=PARAMS,
        name="third",
    )(s0, z, z_even, z_odd, f_near, f_far, w1x, w2x, w2tx, w1tx, b2b)

    final, grad = pl.pallas_call(
        fourth_kernel,
        out_shape=(shape(Q, 2, 8, W), shape(Q, 2, 8, W)),
        compiler_params=PARAMS,
        cost_estimate=pl.CostEstimate(flops=10**9, bytes_accessed=10**6, transcendentals=0),
        name="fourth",
    )(z, p3, g)

    along_x, along_z, along_y = sum_groups()
    sums = spread(sums, along_x).sum(0)
    sums = spread(sums, along_z).sum(0)
    grad_w_in_t, grad_b_in, grad_w_out, grad_b_out = pl.pallas_call(
        last_kernel,
        out_shape=(shape(Q, HID), shape(1, HID), shape(Q, HID), shape(1, Q)),
        compiler_params=PARAMS,
        name="last",
    )(spread(sums, along_y))
    return final, grad, grad_w_in_t.T, grad_b_in[0], grad_w_out, grad_b_out[0]


def solution(mesh):
    return jax.shard_map(
        on_device,
        mesh=mesh,
        in_specs=(
            P(None, "gx", "gy", None),
            P(None, "gx", "gy", None),
            P("gx", "gy", None),
            P(),
            P(),
            P(),
            P(),
        ),
        out_specs=(P(None, "gx", "gy", None), P(None, "gx", "gy", None), P(), P(), P(), P()),
        check_vma=False,
    )
```

```python
import functools
import math

import jax
import jax.numpy as jnp
from jax import lax
from jax.experimental import pallas as pl
from jax.experimental.pallas import tpu as pltpu
from jax.sharding import PartitionSpec as P

Q = 19
HID = 64
T = 24
ONE = 19
W = 128

velocities = (
    (0, 0, 0),
    (1, 0, 0),
    (-1, 0, 0),
    (0, 1, 0),
    (0, -1, 0),
    (0, 0, 1),
    (0, 0, -1),
    (1, 1, 0),
    (-1, -1, 0),
    (1, -1, 0),
    (-1, 1, 0),
    (1, 0, 1),
    (-1, 0, -1),
    (1, 0, -1),
    (-1, 0, 1),
    (0, 1, 1),
    (0, -1, -1),
    (0, 1, -1),
    (0, -1, 1),
)
opposite = (0, 2, 1, 4, 3, 6, 5, 8, 7, 10, 9, 12, 11, 14, 13, 16, 15, 18, 17)

order = tuple(sorted(range(Q), key=lambda k: -velocities[k][0]))
place = {k: i for i, k in enumerate(order)}
UNITS = 2 * Q + 1
SOLID = 2 * Q


def y_pieces(way):
    pieces = []
    for plane in range(2):
        for k in range(Q):
            pieces.append((plane, place[k], 3 + way * velocities[k][1]))
        for k in range(Q):
            pieces.append((plane, Q + place[k], 2 - way * velocities[k][1]))
        pieces.append((plane, SOLID, 3))
    return pieces


Y_ROWS = 200


def split(a):
    high = a.astype(jnp.bfloat16).astype(jnp.float32)
    return high, a - high


def stack3(high, low):
    parts = [high, low, high]
    if (3 * high.shape[0]) % 16:
        parts.append(jnp.zeros((8, high.shape[1]), jnp.float32))
    return jnp.concatenate(parts, axis=0).astype(jnp.bfloat16)


def weights3(a):
    high, low = split(a)
    parts = [high, high, low]
    if (3 * a.shape[1]) % 16:
        parts.append(jnp.zeros((a.shape[0], 8), jnp.float32))
    return jnp.concatenate(parts, axis=1)


def weights2(a):
    high, low = split(a)
    top = jnp.concatenate([high, high], axis=1)
    bottom = jnp.concatenate([low, jnp.zeros_like(low)], axis=1)
    return jnp.concatenate([top, bottom], axis=0)


def mm2(weights, parts):
    both = mm(weights, jnp.concatenate(parts, axis=0).astype(jnp.bfloat16))
    return both[0:T] + both[T:]


def mm(a, b):
    return lax.dot_general(a, b, (((1,), (0,)), ((), ())), preferred_element_type=jnp.float32)


def mm_t(a, b):
    return lax.dot_general(a, b, (((1,), (1,)), ((), ())), preferred_element_type=jnp.float32)


def load_rows(ref, plane, first, count):
    return jnp.concatenate(
        [ref[plane, (first + i) * T : (first + i + 1) * T, :] for i in range(count)], axis=1
    )


def store_rows(ref, plane, first, count, value):
    for i in range(count):
        ref[plane, (first + i) * T : (first + i + 1) * T, :] = value[:, i * W : (i + 1) * W]


def get8(ref, plane, first, k):
    return ref[plane, pl.ds(first * T + k, 8, stride=T), :]


def put8(ref, plane, first, k, value):
    ref[plane, pl.ds(first * T + k, 8, stride=T), :] = value


def z_shift(value, step):
    if step == 0:
        return value
    return pltpu.roll(value, step % W, axis=1)


def pad_tile():
    row = lax.broadcasted_iota(jnp.int32, (8, W), 0)
    return jnp.where(row == ONE - 16, 1.0, 0.0).astype(jnp.float32)


def pad_rows(ref, plane, first, count):
    tile = pad_tile()
    for i in range(count):
        ref[plane, (first + i) * T + 16 : (first + i + 1) * T, :] = tile


def chunks(count, size):
    return [(i, min(size, count - i)) for i in range(0, count, size)]


def first_kernel(
    start_hbm, adjoint_hbm, solid_hbm, w_in_t_hbm, b_in_hbm, w_out_hbm, b_out_hbm,
    z, to_even, to_odd, s0, w1x, w2x, w2tx, w1tx, b2b,
    p1, sq, start, adjoint, solid, w_in_t, b_in, w_out, b_out, sems,
):
    pairs = (
        (w_in_t_hbm, w_in_t), (b_in_hbm, b_in), (w_out_hbm, w_out), (b_out_hbm, b_out),
        (start_hbm, start), (solid_hbm, solid), (adjoint_hbm, adjoint),
    )
    copies = [pltpu.make_async_copy(a, b, sems.at[i]) for i, (a, b) in enumerate(pairs)]
    for copy in copies:
        copy.start()
    sq[...] = jnp.zeros((128, 128), jnp.float32)
    for plane in range(2):
        pad_rows(s0, plane, 0, 8)
    for copy in copies[:4]:
        copy.wait()
    sq[0:Q, 0:HID] = w_in_t[...]
    sq[ONE : ONE + 1, 0:HID] = b_in[...]
    a1t = sq[0:T, 0:HID]
    a1 = sq[...].T[0:HID, 0:T]
    sq[...] = jnp.zeros((128, 128), jnp.float32)
    sq[0:Q, 0:HID] = w_out[...]
    a2 = sq[0:T, 0:HID]
    a2t = sq[...].T[0:HID, 0:T]
    sq[...] = jnp.zeros((128, 128), jnp.float32)
    sq[0:1, 0:Q] = b_out[...]
    b2 = jnp.broadcast_to(sq[...].T[0:T, 0:1], (T, W))
    w1 = weights3(a1)
    w2 = weights2(a2)
    w1x[...] = w1
    w2x[...] = w2
    w2tx[...] = weights3(a2t)
    w1tx[...] = weights2(a1t)
    b2b[...] = b2
    w1 = w1.astype(jnp.bfloat16)
    w2 = w2.astype(jnp.bfloat16)
    for copy in copies[4:]:
        copy.wait()
    for plane in range(2):
        for k in range(Q):
            put8(s0, plane, 0, k, start[k, plane])
        sol = solid[plane].astype(jnp.float32)
        z[plane, SOLID] = sol
        mask = sol > 0.5
        for k in range(Q):
            z[plane, Q + place[k]] = jnp.where(
                mask, adjoint[opposite[k], plane], adjoint[k, plane]
            )
    state = jnp.concatenate([load_rows(s0, plane, 0, 8) for plane in range(2)], axis=1)
    hidden = jnp.tanh(mm(w1, stack3(*split(state))))
    change = mm2(w2, split(hidden))
    for i in range(16):
        plane, y = divmod(i, 8)
        fluid = 1.0 - solid[plane, y : y + 1, :].astype(jnp.float32)
        p1[plane, y * T : (y + 1) * T, :] = state[:, i * W : (i + 1) * W] + fluid * (
            change[:, i * W : (i + 1) * W] + b2
        )
    for plane in range(2):
        for k in range(Q):
            z[plane, place[k]] = get8(p1, plane, 0, k)

    def pack(ref, way):
        at = 0
        for plane, unit, rows in y_pieces(way):
            begin = 8 - rows if way == 1 else 0
            ref[at : at + rows, :] = z[plane, unit, begin : begin + rows, :]
            at += rows
        ref[at:, :] = jnp.zeros((Y_ROWS - at, W), jnp.float32)

    odd = lax.rem(lax.axis_index("gy"), 2)

    @pl.when(odd == 0)
    def _():
        pack(to_even, 1)
        pack(to_odd, -1)

    @pl.when(odd == 1)
    def _():
        pack(to_even, -1)
        pack(to_odd, 1)


def near_kernel(z_own, z):
    z[...] = z_own[...]


def second_kernel(z_own, from_even, from_odd, z, next_rows, to_near, to_far):
    z[:, :, 4:12, :] = z_own[...]

    def unpack(below, above):
        for ref, way in ((below, 1), (above, -1)):
            at = 0
            for plane, unit, rows in y_pieces(way):
                begin = 4 - rows if way == 1 else 12
                z[plane, unit, begin : begin + rows, :] = ref[at : at + rows, :]
                at += rows
        next_rows[OWN : OWN + Y_ROWS, :] = below[...]
        next_rows[OWN + Y_ROWS :, :] = above[...]

    for plane in range(2):
        for unit in range(UNITS):
            at = (plane * UNITS + unit) * 8
            next_rows[at : at + 8, :] = z_own[plane, unit]

    odd = lax.rem(lax.axis_index("gy"), 2)

    @pl.when(odd == 0)
    def _():
        unpack(from_odd, from_even)

    @pl.when(odd == 1)
    def _():
        unpack(from_even, from_odd)

    def pack(ref, way):
        at = 0
        for plane, unit, begin, rows in far_pieces(way):
            ref[at : at + rows, :] = z[plane, unit, begin : begin + rows, :]
            at += rows
        ref[at:, :] = jnp.zeros((FAR_ROWS - at, W), jnp.float32)

    low = lax.rem(lax.axis_index("gx"), 4) < 2

    @pl.when(low)
    def _():
        pack(to_near, 1)
        pack(to_far, -1)

    @pl.when(jnp.logical_not(low))
    def _():
        pack(to_near, -1)
        pack(to_far, 1)


def far_runs(way):
    if way == 1:
        return ((5, 0, 0), (14, 1, 0), (5, 1, Q + 14), (1, 1, SOLID))
    return ((5, 1, 14), (14, 0, 5), (5, 0, Q), (1, 0, SOLID))


def far_pieces(way):
    below = {piece[:2]: piece[2] for piece in y_pieces(1)}
    above = {piece[:2]: piece[2] for piece in y_pieces(-1)}
    units = [(plane, first + i) for count, plane, first in far_runs(way) for i in range(count)]
    pieces = [(plane, unit, 4, 8) for plane, unit in units]
    for key in units:
        pieces.append((*key, 4 - below[key], below[key]))
        pieces.append((*key, 12, above[key]))
    return pieces


FAR_ROWS = 344
OWN = 2 * UNITS * 8


def hold_kernel(f_far, z_odd, token):
    del f_far, z_odd
    token[...] = jnp.zeros(token.shape, jnp.float32)


PLANES = 10
ROWS = 16


def third_kernel(
    scale,
    s0, z_own, z_even, z_odd, f_near, f_far, w1x, w2x, w2tx, w1tx, b2b, token,
    final_hbm, grad_hbm, sums,
    final, grad, out_sems, zs, s1, p2, s2, p3, gp, g, acc1, acc2, sems,
):
    index = lax.axis_index("gx")
    odd = lax.rem(index, 2)
    low = lax.rem(index, 4) < 2
    del token
    copies = [(z_even, zs.at[pl.ds(6 - 4 * odd, 2)]), (z_own, zs.at[4:6])]
    copies = [pltpu.make_async_copy(a, b, sems.at[i]) for i, (a, b) in enumerate(copies)]
    for copy in copies:
        copy.start()

    w1 = w1x[...].astype(jnp.bfloat16)
    w2 = w2x[...].astype(jnp.bfloat16)
    w2t = w2tx[...].astype(jnp.bfloat16)
    w1t = w1tx[...].astype(jnp.bfloat16)
    b2 = b2b[...]
    acc1[...] = jnp.zeros(acc1.shape, jnp.float32)
    acc2[...] = jnp.zeros(acc2.shape, jnp.float32)
    for ref, planes in ((s1, 8), (s2, 6)):
        for plane in range(planes):
            pad_rows(ref, plane, 0, ROWS)
    for plane in range(6):
        for i in range(ROWS):
            gp[plane, i * T + 16 : (i + 1) * T, :] = jnp.zeros((8, W), jnp.float32)

    for plane in range(2):
        for unit in range(UNITS):
            at = (plane * UNITS + unit) * 8
            zs[2 + 4 * odd + plane, unit, 4:12, :] = z_odd[at : at + 8, :]
    for way, at in ((1, OWN), (-1, OWN + Y_ROWS)):
        for plane, unit, count in y_pieces(way):
            begin = 4 - count if way == 1 else 12
            zs[2 + 4 * odd + plane, unit, begin : begin + count, :] = z_odd[at : at + count, :]
            at += count

    def unpack(left, right):
        for ref, way, base in ((left, 1, 0), (right, -1, 8)):
            at = 0
            for plane, unit, begin, count in far_pieces(way):
                zs[base + plane, unit, begin : begin + count, :] = ref[at : at + count, :]
                at += count

    @pl.when(low)
    def _():
        unpack(f_far, f_near)

    @pl.when(jnp.logical_not(low))
    def _():
        unpack(f_near, f_far)

    for copy in copies:
        copy.wait()

    def fluid_rows(x, y):
        return 1.0 - zs[x, SOLID, y : y + 1, :]

    def forward_hidden(state_parts):
        return jnp.tanh(mm(w1, stack3(*state_parts)))

    def collide(p_ref, p_plane, zx, first, count, state, hidden_parts):
        change = mm2(w2, hidden_parts)
        for i in range(count):
            y = first + i
            p_ref[p_plane, y * T : (y + 1) * T, :] = state[:, i * W : (i + 1) * W] + fluid_rows(
                zx, y
            ) * (change[:, i * W : (i + 1) * W] + b2)

    def backward(own, zx, first, count, state_parts, hidden, hidden_parts, grad_post):
        change = jnp.concatenate(
            [
                fluid_rows(zx, first + i) * grad_post[:, i * W : (i + 1) * W]
                for i in range(count)
            ],
            axis=1,
        )
        change_parts = split(change)
        grad_hidden = mm(w2t, stack3(*change_parts))
        grad_pre = grad_hidden * (1.0 - hidden * hidden)
        pre_parts = split(grad_pre)
        back = grad_post + mm2(w1t, pre_parts)
        low = max(first, 4)
        high = min(first + count, 12)

        if own and high > low:
            part = slice((low - first) * W, (high - first) * W)
            left = jnp.concatenate([a[:, part] for a in state_parts], axis=0)
            right = jnp.concatenate([a[:, part] for a in pre_parts + change_parts], axis=0)
            acc1[...] += mm_t(left.astype(jnp.bfloat16), right.astype(jnp.bfloat16))
            left = jnp.concatenate([a[:, part] for a in change_parts], axis=0)
            right = jnp.concatenate([a[:, part] for a in hidden_parts], axis=0)
            acc2[...] += mm_t(left.astype(jnp.bfloat16), right.astype(jnp.bfloat16))
        return back

    def over_planes(halo, body):
        if halo:
            lax.fori_loop(
                0,
                2 * halo,
                lambda i, c: body(False, jnp.where(i < halo, i, i + 2), c),
                0,
                unroll=2 * halo,
            )
        lax.fori_loop(0, 2, lambda i, c: body(True, i + halo, c), 0, unroll=2)

    def reflect(values, mask):
        return [jnp.where(mask, values[opposite[k]], values[k]) for k in range(Q)]

    def stage1(j, carry):
        zx = j + 1
        for y in (1, 7):
            moved = []
            for k in range(Q):
                cx, cy, cz = velocities[k]
                moved.append(z_shift(zs[zx - cx, place[k], y - cy : y - cy + 8, :], cz))
            moved = reflect(moved, zs[zx, SOLID, y : y + 8, :] > 0.5)
            for k in range(Q):
                put8(s1, j, y, k, moved[k])
        for first, count in chunks(14, 14):
            first += 1
            state = load_rows(s1, j, first, count)
            hidden = forward_hidden(split(state))
            collide(p2, j, zx, first, count, state, split(hidden))
        return carry

    lax.fori_loop(0, 8, stage1, 0, unroll=8)

    def stage2(own, j, carry):
        zx = j + 2
        for y in (2, 6):
            moved = []
            for k in range(Q):
                cx, cy, cz = velocities[k]
                moved.append(z_shift(get8(p2, j + 1 - cx, y - cy, k), cz))
            moved = reflect(moved, zs[zx, SOLID, y : y + 8, :] > 0.5)
            for k in range(Q):
                put8(s2, j, y, k, moved[k])
            for k in range(Q):
                cx, cy, cz = velocities[k]
                value = zs[zx + cx, Q + place[k], y + cy : y + cy + 8, :]
                put8(gp, j, y, k, z_shift(value, -cz))
        for first, count in chunks(12, 12):
            first += 2
            state = load_rows(s2, j, first, count)
            state_parts = split(state)
            hidden = forward_hidden(state_parts)
            hidden_parts = split(hidden)
            collide(p3, j, zx, first, count, state, hidden_parts)
            grad_post = load_rows(gp, j, first, count)
            back = backward(own, zx, first, count, state_parts, hidden, hidden_parts, grad_post)
            store_rows(g, j, first, count, back)
        return carry

    over_planes(2, stage2)

    for plane in range(2):
        moved = []
        for k in range(Q):
            cx, cy, cz = velocities[k]
            moved.append(z_shift(get8(p3, plane + 2 - cx, 4 - cy, k), cz))
        moved = reflect(moved, zs[plane + 4, SOLID, 4:12, :] > 0.5)
        for k in range(Q):
            final[k, plane] = moved[k]
    final_copy = pltpu.make_async_copy(final, final_hbm, out_sems.at[0])
    final_copy.start()

    def run_back(g_ref, g_plane, zx, y, out_plane):
        for k in range(Q):
            cx, cy, cz = velocities[k]
            one = get8(g_ref, g_plane + cx, y + cy, k)
            if k != 0:
                other = get8(g_ref, g_plane + cx, y + cy, opposite[k])
                mask = zs[zx + cx, SOLID, y + cy : y + cy + 8, :] > 0.5
                one = jnp.where(mask, other, one)
            put8(gp, out_plane, y, k, z_shift(one, -cz))

    def stage3(own, j, carry):
        zx = j + 3
        for y in (3, 5):
            run_back(g, j + 1, zx, y, j)
        for first, count in ((3, 10),):
            state_parts = split(load_rows(s1, j + 2, first, count))
            hidden = forward_hidden(state_parts)
            grad_post = load_rows(gp, j, first, count)
            back = backward(own, zx, first, count, state_parts, hidden, split(hidden), grad_post)
            store_rows(p2, j, first, count, back)
        return carry

    over_planes(1, stage3)

    def stage4(own, j, carry):
        zx = j + 4
        run_back(p2, j + 1, zx, 4, j)
        for first, count in ((4, 8),):
            state_parts = split(load_rows(s0, j, first - 4, count))
            hidden = forward_hidden(state_parts)
            grad_post = load_rows(gp, j, first, count)
            back = backward(own, zx, first, count, state_parts, hidden, split(hidden), grad_post)
            store_rows(g, j, first, count, back)
        for k in range(Q):
            grad[k, j] = get8(g, j, 4, k)
        return carry

    over_planes(0, stage4)
    grad_copy = pltpu.make_async_copy(grad, grad_hbm, out_sems.at[1])
    grad_copy.start()

    one = acc1[0:T, :] + acc1[T : 2 * T, :]
    two = acc2[0:T, :] + acc2[T : 2 * T, :]
    in_part = one[:, 0:HID] + one[:, HID : 2 * HID]
    out_part = two[:, 0:HID] + two[:, HID : 2 * HID]
    bias = one[:, 2 * HID : 2 * HID + T] + one[:, 2 * HID + T : 2 * HID + 2 * T]
    sums[...] = jnp.zeros(sums.shape, jnp.float32)
    sums[0:T, 0:HID] = in_part * scale
    sums[0:Q, HID : 2 * HID] = out_part[0:Q, :] * scale
    sums[ONE : ONE + 1, HID : HID + T] = bias[ONE : ONE + 1, :] * scale
    final_copy.wait()
    grad_copy.wait()


def last_kernel(parts, grad_w_in_t, grad_b_in, grad_w_out, grad_b_out):
    total = parts[0]
    for i in range(1, parts.shape[0]):
        total = total + parts[i]
    grad_w_in_t[...] = total[0:Q, 0:HID]
    grad_b_in[...] = total[ONE : ONE + 1, 0:HID]
    grad_w_out[...] = total[0:Q, HID : 2 * HID]
    grad_b_out[...] = total[ONE : ONE + 1, HID : HID + Q]


def swap_even(x, axis, step=1):
    count = lax.axis_size(axis)
    return lax.ppermute(x, axis, [(i, i ^ step) for i in range(count)])


def swap_odd(x, axis, step=1):
    count = lax.axis_size(axis)
    return lax.ppermute(
        x, axis, [(i, (i + step if i & step else i - step) % count) for i in range(count)]
    )


def spread(x, groups):
    count = len(groups[0])
    return lax.all_to_all(
        jnp.broadcast_to(x[None], (count,) + x.shape), ("gx", "gy"), 0, 0, axis_index_groups=groups
    )


def sum_groups():
    gx, gy = lax.axis_size("gx"), lax.axis_size("gy")
    nx, ny = math.gcd(gx, 8), math.gcd(gy, 8)
    zs = [(a, b) for b in range(gy // ny) for a in range(gx // nx)]

    def at(z, x, y):
        return (z[0] * nx + x) * gy + z[1] * ny + y

    return (
        [[at(z, x, y) for x in range(nx)] for z in zs for y in range(ny)],
        [[at(z, x, y) for z in zs] for x in range(nx) for y in range(ny)],
        [[at(z, x, y) for y in range(ny)] for z in zs for x in range(nx)],
    )


F32 = jnp.float32


def shape(*dims):
    return jax.ShapeDtypeStruct(dims, F32)


FIRST_VMEM = 63 * 1024 * 1024
PARAMS = pltpu.CompilerParams(vmem_limit_bytes=48 * 1024 * 1024)


def on_device(start, adjoint, solid, w_in, b_in, w_out, b_out):
    rows = pltpu.VMEM
    z, to_even, to_odd, s0, w1x, w2x, w2tx, w1tx, b2b = pl.pallas_call(
        first_kernel,
        out_shape=(
            shape(2, UNITS, 8, W),
            shape(Y_ROWS, W),
            shape(Y_ROWS, W),
            shape(2, 8 * T, W),
            shape(HID, 80),
            shape(2 * T, 2 * HID),
            shape(HID, 80),
            shape(2 * T, 2 * HID),
            shape(T, W),
        ),
        in_specs=[pl.BlockSpec(memory_space=pltpu.HBM)] * 7,
        scratch_shapes=[
            rows((2, 8 * T, W), F32),
            rows((128, 128), F32),
            rows((Q, 2, 8, W), F32),
            rows((Q, 2, 8, W), F32),
            rows((2, 8, W), jnp.int32),
            rows((Q, HID), F32),
            rows((1, HID), F32),
            rows((Q, HID), F32),
            rows((1, Q), F32),
            pltpu.SemaphoreType.DMA((7,)),
        ],
        compiler_params=pltpu.CompilerParams(vmem_limit_bytes=FIRST_VMEM),
        name="first",
    )(start, adjoint, solid, w_in.T, b_in.reshape(1, HID), w_out, b_out.reshape(1, Q))

    from_even = swap_even(to_even, "gy")
    from_odd = swap_odd(to_odd, "gy")

    z = pl.pallas_call(
        near_kernel,
        out_shape=shape(2, UNITS, 8, W),
        compiler_params=PARAMS,
        name="near",
    )(z)
    z, next_rows, to_near, to_far = pl.pallas_call(
        second_kernel,
        out_shape=(
            shape(2, UNITS, ROWS, W),
            shape(OWN + 2 * Y_ROWS, W),
            shape(FAR_ROWS, W),
            shape(FAR_ROWS, W),
        ),
        compiler_params=PARAMS,
        name="second",
    )(z, from_even, from_odd)

    z_odd = swap_odd(next_rows, "gx")
    f_far = swap_odd(to_far, "gx", 2)
    f_near = swap_even(to_near, "gx", 2)
    z_even = swap_even(z, "gx")

    token = pl.pallas_call(
        hold_kernel,
        out_shape=shape(8, W),
        in_specs=[pl.BlockSpec(memory_space=pl.ANY)] * 2,
        compiler_params=PARAMS,
        cost_estimate=pl.CostEstimate(flops=6 * 10**9, bytes_accessed=10**6, transcendentals=0),
        name="hold",
    )(f_far, z_odd)

    cells = 16 * W * lax.axis_size("gx") * lax.axis_size("gy")
    vmem = pl.BlockSpec(memory_space=pltpu.VMEM)
    hbm = pl.BlockSpec(memory_space=pl.ANY)
    final, grad, sums = pl.pallas_call(
        functools.partial(third_kernel, 1.0 / math.sqrt(cells)),
        out_shape=(shape(Q, 2, 8, W), shape(Q, 2, 8, W), shape(T, W)),
        in_specs=[vmem] + [hbm] * 2 + [vmem] * 8 + [hbm],
        out_specs=(hbm, hbm, vmem),
        scratch_shapes=[
            rows((Q, 2, 8, W), F32),
            rows((Q, 2, 8, W), F32),
            pltpu.SemaphoreType.DMA((2,)),
            rows((PLANES, UNITS, ROWS, W), F32),
            rows((8, ROWS * T, W), F32),
            rows((8, ROWS * T, W), F32),
            rows((6, ROWS * T, W), F32),
            rows((6, ROWS * T, W), F32),
            rows((6, ROWS * T, W), F32),
            rows((6, ROWS * T, W), F32),
            rows((2 * T, 2 * HID + 2 * T), F32),
            rows((2 * T, 2 * HID), F32),
            pltpu.SemaphoreType.DMA((2,)),
        ],
        compiler_params=PARAMS,
        name="third",
    )(s0, z, z_even, z_odd, f_near, f_far, w1x, w2x, w2tx, w1tx, b2b, token)

    along_x, along_z, along_y = sum_groups()
    sums = spread(sums, along_x).sum(0)
    sums = spread(sums, along_z).sum(0)
    grad_w_in_t, grad_b_in, grad_w_out, grad_b_out = pl.pallas_call(
        last_kernel,
        out_shape=(shape(Q, HID), shape(1, HID), shape(Q, HID), shape(1, Q)),
        compiler_params=PARAMS,
        name="last",
    )(spread(sums, along_y))
    return final, grad, grad_w_in_t.T, grad_b_in[0], grad_w_out, grad_b_out[0]


def solution(mesh):
    return jax.shard_map(
        on_device,
        mesh=mesh,
        in_specs=(
            P(None, "gx", "gy", None),
            P(None, "gx", "gy", None),
            P("gx", "gy", None),
            P(),
            P(),
            P(),
            P(),
        ),
        out_specs=(P(None, "gx", "gy", None), P(None, "gx", "gy", None), P(), P(), P(), P()),
        check_vma=False,
    )
```

```python
import functools
import math

import jax
import jax.numpy as jnp
from jax import lax
from jax.experimental import pallas as pl
from jax.experimental.pallas import tpu as pltpu
from jax.sharding import PartitionSpec as P

Q = 19
HID = 64
T = 24
ONE = 19
W = 128

velocities = (
    (0, 0, 0),
    (1, 0, 0),
    (-1, 0, 0),
    (0, 1, 0),
    (0, -1, 0),
    (0, 0, 1),
    (0, 0, -1),
    (1, 1, 0),
    (-1, -1, 0),
    (1, -1, 0),
    (-1, 1, 0),
    (1, 0, 1),
    (-1, 0, -1),
    (1, 0, -1),
    (-1, 0, 1),
    (0, 1, 1),
    (0, -1, -1),
    (0, 1, -1),
    (0, -1, 1),
)
opposite = (0, 2, 1, 4, 3, 6, 5, 8, 7, 10, 9, 12, 11, 14, 13, 16, 15, 18, 17)

order = tuple(sorted(range(Q), key=lambda k: -velocities[k][0]))
place = {k: i for i, k in enumerate(order)}
UNITS = 2 * Q + 1
SOLID = 2 * Q


def y_pieces(way):
    pieces = []
    for plane in range(2):
        for k in range(Q):
            pieces.append((plane, place[k], 3 + way * velocities[k][1]))
        for k in range(Q):
            pieces.append((plane, Q + place[k], 2 - way * velocities[k][1]))
        pieces.append((plane, SOLID, 3))
    return pieces


Y_ROWS = 200


def split(a):
    high = a.astype(jnp.bfloat16).astype(jnp.float32)
    return high, a - high


def stack3(high, low):
    parts = [high, low, high]
    if (3 * high.shape[0]) % 16:
        parts.append(jnp.zeros((8, high.shape[1]), jnp.float32))
    return jnp.concatenate(parts, axis=0).astype(jnp.bfloat16)


def weights3(a):
    high, low = split(a)
    parts = [high, high, low]
    if (3 * a.shape[1]) % 16:
        parts.append(jnp.zeros((a.shape[0], 8), jnp.float32))
    return jnp.concatenate(parts, axis=1)


def weights2(a):
    high, low = split(a)
    top = jnp.concatenate([high, high], axis=1)
    bottom = jnp.concatenate([low, jnp.zeros_like(low)], axis=1)
    return jnp.concatenate([top, bottom], axis=0)


def mm2(weights, parts):
    both = mm(weights, jnp.concatenate(parts, axis=0).astype(jnp.bfloat16))
    return both[0:T] + both[T:]


def mm(a, b):
    return lax.dot_general(a, b, (((1,), (0,)), ((), ())), preferred_element_type=jnp.float32)


def mm_t(a, b):
    return lax.dot_general(a, b, (((1,), (1,)), ((), ())), preferred_element_type=jnp.float32)


def load_rows(ref, plane, first, count):
    return jnp.concatenate(
        [ref[plane, (first + i) * T : (first + i + 1) * T, :] for i in range(count)], axis=1
    )


def store_rows(ref, plane, first, count, value):
    for i in range(count):
        ref[plane, (first + i) * T : (first + i + 1) * T, :] = value[:, i * W : (i + 1) * W]


def get8(ref, plane, first, k):
    return ref[plane, pl.ds(first * T + k, 8, stride=T), :]


def put8(ref, plane, first, k, value):
    ref[plane, pl.ds(first * T + k, 8, stride=T), :] = value


def z_shift(value, step):
    if step == 0:
        return value
    return pltpu.roll(value, step % W, axis=1)


def pad_tile():
    row = lax.broadcasted_iota(jnp.int32, (8, W), 0)
    return jnp.where(row == ONE - 16, 1.0, 0.0).astype(jnp.float32)


def pad_rows(ref, plane, first, count):
    tile = pad_tile()
    for i in range(count):
        ref[plane, (first + i) * T + 16 : (first + i + 1) * T, :] = tile


def chunks(count, size):
    return [(i, min(size, count - i)) for i in range(0, count, size)]


def first_kernel(
    start_hbm, adjoint_hbm, solid_hbm, w_in_t_hbm, b_in_hbm, w_out_hbm, b_out_hbm,
    z, to_even, to_odd, s0, w1x, w2x, w2tx, w1tx, b2b,
    p1, sq, start, adjoint, solid, w_in_t, b_in, w_out, b_out, sems,
):
    pairs = (
        (w_in_t_hbm, w_in_t), (b_in_hbm, b_in), (w_out_hbm, w_out), (b_out_hbm, b_out),
        (start_hbm, start), (solid_hbm, solid), (adjoint_hbm, adjoint),
    )
    copies = [pltpu.make_async_copy(a, b, sems.at[i]) for i, (a, b) in enumerate(pairs)]
    for copy in copies:
        copy.start()
    sq[...] = jnp.zeros((128, 128), jnp.float32)
    for plane in range(2):
        pad_rows(s0, plane, 0, 8)
    for copy in copies[:4]:
        copy.wait()
    sq[0:Q, 0:HID] = w_in_t[...]
    sq[ONE : ONE + 1, 0:HID] = b_in[...]
    a1t = sq[0:T, 0:HID]
    a1 = sq[...].T[0:HID, 0:T]
    sq[...] = jnp.zeros((128, 128), jnp.float32)
    sq[0:Q, 0:HID] = w_out[...]
    a2 = sq[0:T, 0:HID]
    a2t = sq[...].T[0:HID, 0:T]
    sq[...] = jnp.zeros((128, 128), jnp.float32)
    sq[0:1, 0:Q] = b_out[...]
    b2 = jnp.broadcast_to(sq[...].T[0:T, 0:1], (T, W))
    w1 = weights3(a1)
    w2 = weights2(a2)
    w1x[...] = w1
    w2x[...] = w2
    w2tx[...] = weights3(a2t)
    w1tx[...] = weights2(a1t)
    b2b[...] = b2
    w1 = w1.astype(jnp.bfloat16)
    w2 = w2.astype(jnp.bfloat16)
    for copy in copies[4:]:
        copy.wait()
    for plane in range(2):
        for k in range(Q):
            put8(s0, plane, 0, k, start[k, plane])
        sol = solid[plane].astype(jnp.float32)
        z[plane, SOLID] = sol
        mask = sol > 0.5
        for k in range(Q):
            z[plane, Q + place[k]] = jnp.where(
                mask, adjoint[opposite[k], plane], adjoint[k, plane]
            )
    state = jnp.concatenate([load_rows(s0, plane, 0, 8) for plane in range(2)], axis=1)
    hidden = jnp.tanh(mm(w1, stack3(*split(state))))
    change = mm2(w2, split(hidden))
    for i in range(16):
        plane, y = divmod(i, 8)
        fluid = 1.0 - solid[plane, y : y + 1, :].astype(jnp.float32)
        p1[plane, y * T : (y + 1) * T, :] = state[:, i * W : (i + 1) * W] + fluid * (
            change[:, i * W : (i + 1) * W] + b2
        )
    for plane in range(2):
        for k in range(Q):
            z[plane, place[k]] = get8(p1, plane, 0, k)

    def pack(ref, way):
        at = 0
        for plane, unit, rows in y_pieces(way):
            begin = 8 - rows if way == 1 else 0
            ref[at : at + rows, :] = z[plane, unit, begin : begin + rows, :]
            at += rows
        ref[at:, :] = jnp.zeros((Y_ROWS - at, W), jnp.float32)

    odd = lax.rem(lax.axis_index("gy"), 2)

    @pl.when(odd == 0)
    def _():
        pack(to_even, 1)
        pack(to_odd, -1)

    @pl.when(odd == 1)
    def _():
        pack(to_even, -1)
        pack(to_odd, 1)


def near_kernel(z_own, z):
    z[...] = z_own[...]


def second_kernel(z_own, from_even, from_odd, z, next_rows, to_near, to_far):
    z[:, :, 4:12, :] = z_own[...]

    def unpack(below, above):
        for ref, way in ((below, 1), (above, -1)):
            at = 0
            for plane, unit, rows in y_pieces(way):
                begin = 4 - rows if way == 1 else 12
                z[plane, unit, begin : begin + rows, :] = ref[at : at + rows, :]
                at += rows
        next_rows[OWN : OWN + Y_ROWS, :] = below[...]
        next_rows[OWN + Y_ROWS :, :] = above[...]

    for plane in range(2):
        for unit in range(UNITS):
            at = (plane * UNITS + unit) * 8
            next_rows[at : at + 8, :] = z_own[plane, unit]

    odd = lax.rem(lax.axis_index("gy"), 2)

    @pl.when(odd == 0)
    def _():
        unpack(from_odd, from_even)

    @pl.when(odd == 1)
    def _():
        unpack(from_even, from_odd)

    def pack(ref, way):
        at = 0
        for plane, unit, begin, rows in far_pieces(way):
            ref[at : at + rows, :] = z[plane, unit, begin : begin + rows, :]
            at += rows
        ref[at:, :] = jnp.zeros((FAR_ROWS - at, W), jnp.float32)

    low = lax.rem(lax.axis_index("gx"), 4) < 2

    @pl.when(low)
    def _():
        pack(to_near, 1)
        pack(to_far, -1)

    @pl.when(jnp.logical_not(low))
    def _():
        pack(to_near, -1)
        pack(to_far, 1)


def far_runs(way):
    if way == 1:
        return ((5, 0, 0), (14, 1, 0), (5, 1, Q + 14), (1, 1, SOLID))
    return ((5, 1, 14), (14, 0, 5), (5, 0, Q), (1, 0, SOLID))


def far_pieces(way):
    below = {piece[:2]: piece[2] for piece in y_pieces(1)}
    above = {piece[:2]: piece[2] for piece in y_pieces(-1)}
    units = [(plane, first + i) for count, plane, first in far_runs(way) for i in range(count)]
    pieces = [(plane, unit, 4, 8) for plane, unit in units]
    for key in units:
        pieces.append((*key, 4 - below[key], below[key]))
        pieces.append((*key, 12, above[key]))
    return pieces


FAR_ROWS = 344
OWN = 2 * UNITS * 8


def hold_kernel(f_far, z_odd, token):
    del f_far, z_odd
    token[...] = jnp.zeros(token.shape, jnp.float32)


PLANES = 10
ROWS = 16


def third_kernel(
    scale,
    s0, z_own, z_even, z_odd, f_near, f_far, w1x, w2x, w2tx, w1tx, b2b, token,
    final_hbm, grad_hbm, sums,
    packed, final, grad, out_sems, zs, s1, p2, s2, p3, gp, g, acc1, acc2, sems,
):
    index = lax.axis_index("gx")
    odd = lax.rem(index, 2)
    low = lax.rem(index, 4) < 2
    del token
    copies = [(z_even, zs.at[pl.ds(6 - 4 * odd, 2)]), (z_own, zs.at[4:6])]
    copies = [pltpu.make_async_copy(a, b, sems.at[i]) for i, (a, b) in enumerate(copies)]
    for copy in copies:
        copy.start()

    w1 = w1x[...].astype(jnp.bfloat16)
    w2 = w2x[...].astype(jnp.bfloat16)
    w2t = w2tx[...].astype(jnp.bfloat16)
    w1t = w1tx[...].astype(jnp.bfloat16)
    b2 = b2b[...]
    acc1[...] = jnp.zeros(acc1.shape, jnp.float32)
    acc2[...] = jnp.zeros(acc2.shape, jnp.float32)
    for ref, planes in ((s1, 8), (s2, 6)):
        for plane in range(planes):
            pad_rows(ref, plane, 0, ROWS)
    for plane in range(6):
        for i in range(ROWS):
            gp[plane, i * T + 16 : (i + 1) * T, :] = jnp.zeros((8, W), jnp.float32)

    for plane in range(2):
        for unit in range(UNITS):
            at = (plane * UNITS + unit) * 8
            zs[2 + 4 * odd + plane, unit, 4:12, :] = z_odd[at : at + 8, :]
    for way, at in ((1, OWN), (-1, OWN + Y_ROWS)):
        for plane, unit, count in y_pieces(way):
            begin = 4 - count if way == 1 else 12
            zs[2 + 4 * odd + plane, unit, begin : begin + count, :] = z_odd[at : at + count, :]
            at += count

    def unpack(left, right):
        for ref, way, base in ((left, 1, 0), (right, -1, 8)):
            at = 0
            for plane, unit, begin, count in far_pieces(way):
                zs[base + plane, unit, begin : begin + count, :] = ref[at : at + count, :]
                at += count

    @pl.when(low)
    def _():
        unpack(f_far, f_near)

    @pl.when(jnp.logical_not(low))
    def _():
        unpack(f_near, f_far)

    for copy in copies:
        copy.wait()

    def fluid_rows(x, y):
        return 1.0 - zs[x, SOLID, y : y + 1, :]

    def forward_hidden(state_parts):
        return jnp.tanh(mm(w1, stack3(*state_parts)))

    def collide(p_ref, p_plane, zx, first, count, state, hidden_parts):
        change = mm2(w2, hidden_parts)
        for i in range(count):
            y = first + i
            p_ref[p_plane, y * T : (y + 1) * T, :] = state[:, i * W : (i + 1) * W] + fluid_rows(
                zx, y
            ) * (change[:, i * W : (i + 1) * W] + b2)

    def backward(own, zx, first, count, state_parts, hidden, hidden_parts, grad_post):
        change = jnp.concatenate(
            [
                fluid_rows(zx, first + i) * grad_post[:, i * W : (i + 1) * W]
                for i in range(count)
            ],
            axis=1,
        )
        change_parts = split(change)
        grad_hidden = mm(w2t, stack3(*change_parts))
        grad_pre = grad_hidden * (1.0 - hidden * hidden)
        pre_parts = split(grad_pre)
        back = grad_post + mm2(w1t, pre_parts)
        low = max(first, 4)
        high = min(first + count, 12)

        if own and high > low:
            part = slice((low - first) * W, (high - first) * W)
            left = jnp.concatenate([a[:, part] for a in state_parts], axis=0)
            right = jnp.concatenate([a[:, part] for a in pre_parts + change_parts], axis=0)
            acc1[...] += mm_t(left.astype(jnp.bfloat16), right.astype(jnp.bfloat16))
            left = jnp.concatenate([a[:, part] for a in change_parts], axis=0)
            right = jnp.concatenate([a[:, part] for a in hidden_parts], axis=0)
            acc2[...] += mm_t(left.astype(jnp.bfloat16), right.astype(jnp.bfloat16))
        return back

    def over_planes(halo, body):
        if halo:
            lax.fori_loop(
                0,
                2 * halo,
                lambda i, c: body(False, jnp.where(i < halo, i, i + 2), c),
                0,
                unroll=2 * halo,
            )
        lax.fori_loop(0, 2, lambda i, c: body(True, i + halo, c), 0, unroll=2)

    def reflect(values, mask):
        return [jnp.where(mask, values[opposite[k]], values[k]) for k in range(Q)]

    def stage1(j, carry):
        zx = j + 1
        for y in (1, 7):
            moved = []
            for k in range(Q):
                cx, cy, cz = velocities[k]
                moved.append(z_shift(zs[zx - cx, place[k], y - cy : y - cy + 8, :], cz))
            moved = reflect(moved, zs[zx, SOLID, y : y + 8, :] > 0.5)
            for k in range(Q):
                put8(s1, j, y, k, moved[k])
        for first, count in chunks(14, 14):
            first += 1
            state = load_rows(s1, j, first, count)
            hidden = forward_hidden(split(state))
            collide(p2, j, zx, first, count, state, split(hidden))
        return carry

    lax.fori_loop(0, 8, stage1, 0, unroll=8)

    def stage2(own, j, carry):
        zx = j + 2
        for y in (2, 6):
            moved = []
            for k in range(Q):
                cx, cy, cz = velocities[k]
                moved.append(z_shift(get8(p2, j + 1 - cx, y - cy, k), cz))
            moved = reflect(moved, zs[zx, SOLID, y : y + 8, :] > 0.5)
            for k in range(Q):
                put8(s2, j, y, k, moved[k])
            for k in range(Q):
                cx, cy, cz = velocities[k]
                value = zs[zx + cx, Q + place[k], y + cy : y + cy + 8, :]
                put8(gp, j, y, k, z_shift(value, -cz))
        for first, count in chunks(12, 12):
            first += 2
            state = load_rows(s2, j, first, count)
            state_parts = split(state)
            hidden = forward_hidden(state_parts)
            hidden_parts = split(hidden)
            collide(p3, j, zx, first, count, state, hidden_parts)
            grad_post = load_rows(gp, j, first, count)
            back = backward(own, zx, first, count, state_parts, hidden, hidden_parts, grad_post)
            store_rows(g, j, first, count, back)
        return carry

    over_planes(2, stage2)

    for plane in range(2):
        moved = []
        for k in range(Q):
            cx, cy, cz = velocities[k]
            moved.append(z_shift(get8(p3, plane + 2 - cx, 4 - cy, k), cz))
        moved = reflect(moved, zs[plane + 4, SOLID, 4:12, :] > 0.5)
        for k in range(Q):
            final[k, plane] = moved[k]
    final_copy = pltpu.make_async_copy(final, final_hbm, out_sems.at[0])
    final_copy.start()

    def run_back(g_ref, g_plane, zx, y, out_plane):
        for k in range(Q):
            cx, cy, cz = velocities[k]
            one = get8(g_ref, g_plane + cx, y + cy, k)
            if k != 0:
                other = get8(g_ref, g_plane + cx, y + cy, opposite[k])
                mask = zs[zx + cx, SOLID, y + cy : y + cy + 8, :] > 0.5
                one = jnp.where(mask, other, one)
            put8(gp, out_plane, y, k, z_shift(one, -cz))

    def stage3(own, j, carry):
        zx = j + 3
        for y in (3, 5):
            run_back(g, j + 1, zx, y, j)
        for first, count in ((3, 10),):
            state_parts = split(load_rows(s1, j + 2, first, count))
            hidden = forward_hidden(state_parts)
            grad_post = load_rows(gp, j, first, count)
            back = backward(own, zx, first, count, state_parts, hidden, split(hidden), grad_post)
            store_rows(p2, j, first, count, back)
        return carry

    over_planes(1, stage3)

    def stage4(own, j, carry):
        zx = j + 4
        run_back(p2, j + 1, zx, 4, j)
        for first, count in ((4, 8),):
            state_parts = split(load_rows(s0, j, first - 4, count))
            hidden = forward_hidden(state_parts)
            grad_post = load_rows(gp, j, first, count)
            back = backward(own, zx, first, count, state_parts, hidden, split(hidden), grad_post)
            store_rows(g, j, first, count, back)
        for k in range(Q):
            grad[k, j] = get8(g, j, 4, k)
        return carry

    over_planes(0, stage4)
    grad_copy = pltpu.make_async_copy(grad, grad_hbm, out_sems.at[1])
    grad_copy.start()

    one = acc1[0:T, :] + acc1[T : 2 * T, :]
    two = acc2[0:T, :] + acc2[T : 2 * T, :]
    in_part = one[:, 0:HID] + one[:, HID : 2 * HID]
    out_part = two[:, 0:HID] + two[:, HID : 2 * HID]
    bias = one[:, 2 * HID : 2 * HID + T] + one[:, 2 * HID + T : 2 * HID + 2 * T]
    packed[...] = jnp.zeros(packed.shape, jnp.float32)
    packed[0:T, 0:HID] = in_part * scale
    packed[0:Q, HID : 2 * HID] = out_part[0:Q, :] * scale
    packed[ONE : ONE + 1, HID : HID + T] = bias[ONE : ONE + 1, :] * scale
    for i in range(ONE + 1):
        sums[i] = packed[i : i + 1, :]
    final_copy.wait()
    grad_copy.wait()


def last_kernel(parts, grad_w_in_t, grad_b_in, grad_w_out, grad_b_out):
    for row in range(ONE + 1):
        total = parts[0, row]
        for i in range(1, parts.shape[0]):
            total = total + parts[i, row]
        if row < Q:
            grad_w_in_t[row : row + 1, :] = total[:, 0:HID]
            grad_w_out[row : row + 1, :] = total[:, HID : 2 * HID]
        else:
            grad_b_in[...] = total[:, 0:HID]
            grad_b_out[...] = total[:, HID : HID + Q]


def swap_even(x, axis, step=1):
    count = lax.axis_size(axis)
    return lax.ppermute(x, axis, [(i, i ^ step) for i in range(count)])


def swap_odd(x, axis, step=1):
    count = lax.axis_size(axis)
    return lax.ppermute(
        x, axis, [(i, (i + step if i & step else i - step) % count) for i in range(count)]
    )


def spread(x, groups):
    count = len(groups[0])
    return lax.all_to_all(
        jnp.broadcast_to(x[None], (count,) + x.shape), ("gx", "gy"), 0, 0, axis_index_groups=groups
    )


def sum_groups():
    gx, gy = lax.axis_size("gx"), lax.axis_size("gy")
    nx, ny = math.gcd(gx, 8), math.gcd(gy, 8)
    zs = [(a, b) for b in range(gy // ny) for a in range(gx // nx)]

    def at(z, x, y):
        return (z[0] * nx + x) * gy + z[1] * ny + y

    return (
        [[at(z, x, y) for x in range(nx)] for z in zs for y in range(ny)],
        [[at(z, x, y) for z in zs] for x in range(nx) for y in range(ny)],
        [[at(z, x, y) for y in range(ny)] for z in zs for x in range(nx)],
    )


F32 = jnp.float32


def shape(*dims):
    return jax.ShapeDtypeStruct(dims, F32)


FIRST_VMEM = 63 * 1024 * 1024
PARAMS = pltpu.CompilerParams(vmem_limit_bytes=48 * 1024 * 1024)


def on_device(start, adjoint, solid, w_in, b_in, w_out, b_out):
    rows = pltpu.VMEM
    z, to_even, to_odd, s0, w1x, w2x, w2tx, w1tx, b2b = pl.pallas_call(
        first_kernel,
        out_shape=(
            shape(2, UNITS, 8, W),
            shape(Y_ROWS, W),
            shape(Y_ROWS, W),
            shape(2, 8 * T, W),
            shape(HID, 80),
            shape(2 * T, 2 * HID),
            shape(HID, 80),
            shape(2 * T, 2 * HID),
            shape(T, W),
        ),
        in_specs=[pl.BlockSpec(memory_space=pltpu.HBM)] * 7,
        scratch_shapes=[
            rows((2, 8 * T, W), F32),
            rows((128, 128), F32),
            rows((Q, 2, 8, W), F32),
            rows((Q, 2, 8, W), F32),
            rows((2, 8, W), jnp.int32),
            rows((Q, HID), F32),
            rows((1, HID), F32),
            rows((Q, HID), F32),
            rows((1, Q), F32),
            pltpu.SemaphoreType.DMA((7,)),
        ],
        compiler_params=pltpu.CompilerParams(vmem_limit_bytes=FIRST_VMEM),
        name="first",
    )(start, adjoint, solid, w_in.T, b_in.reshape(1, HID), w_out, b_out.reshape(1, Q))

    from_even = swap_even(to_even, "gy")
    from_odd = swap_odd(to_odd, "gy")

    z = pl.pallas_call(
        near_kernel,
        out_shape=shape(2, UNITS, 8, W),
        compiler_params=PARAMS,
        name="near",
    )(z)
    z, next_rows, to_near, to_far = pl.pallas_call(
        second_kernel,
        out_shape=(
            shape(2, UNITS, ROWS, W),
            shape(OWN + 2 * Y_ROWS, W),
            shape(FAR_ROWS, W),
            shape(FAR_ROWS, W),
        ),
        compiler_params=PARAMS,
        name="second",
    )(z, from_even, from_odd)

    z_odd = swap_odd(next_rows, "gx")
    f_far = swap_odd(to_far, "gx", 2)
    f_near = swap_even(to_near, "gx", 2)
    z_even = swap_even(z, "gx")

    token = pl.pallas_call(
        hold_kernel,
        out_shape=shape(8, W),
        in_specs=[pl.BlockSpec(memory_space=pl.ANY)] * 2,
        compiler_params=PARAMS,
        cost_estimate=pl.CostEstimate(flops=6 * 10**9, bytes_accessed=10**6, transcendentals=0),
        name="hold",
    )(f_far, z_odd)

    cells = 16 * W * lax.axis_size("gx") * lax.axis_size("gy")
    vmem = pl.BlockSpec(memory_space=pltpu.VMEM)
    hbm = pl.BlockSpec(memory_space=pl.ANY)
    final, grad, sums = pl.pallas_call(
        functools.partial(third_kernel, 1.0 / math.sqrt(cells)),
        out_shape=(shape(Q, 2, 8, W), shape(Q, 2, 8, W), shape(ONE + 1, 1, W)),
        in_specs=[vmem] + [hbm] * 2 + [vmem] * 8 + [hbm],
        out_specs=(hbm, hbm, vmem),
        scratch_shapes=[
            rows((T, W), F32),
            rows((Q, 2, 8, W), F32),
            rows((Q, 2, 8, W), F32),
            pltpu.SemaphoreType.DMA((2,)),
            rows((PLANES, UNITS, ROWS, W), F32),
            rows((8, ROWS * T, W), F32),
            rows((8, ROWS * T, W), F32),
            rows((6, ROWS * T, W), F32),
            rows((6, ROWS * T, W), F32),
            rows((6, ROWS * T, W), F32),
            rows((6, ROWS * T, W), F32),
            rows((2 * T, 2 * HID + 2 * T), F32),
            rows((2 * T, 2 * HID), F32),
            pltpu.SemaphoreType.DMA((2,)),
        ],
        compiler_params=PARAMS,
        name="third",
    )(s0, z, z_even, z_odd, f_near, f_far, w1x, w2x, w2tx, w1tx, b2b, token)

    along_x, along_z, along_y = sum_groups()
    sums = spread(sums, along_x).sum(0)
    sums = spread(sums, along_z).sum(0)
    grad_w_in_t, grad_b_in, grad_w_out, grad_b_out = pl.pallas_call(
        last_kernel,
        out_shape=(shape(Q, HID), shape(1, HID), shape(Q, HID), shape(1, Q)),
        compiler_params=PARAMS,
        name="last",
    )(spread(sums, along_y))
    return final, grad, grad_w_in_t.T, grad_b_in[0], grad_w_out, grad_b_out[0]


def solution(mesh):
    return jax.shard_map(
        on_device,
        mesh=mesh,
        in_specs=(
            P(None, "gx", "gy", None),
            P(None, "gx", "gy", None),
            P("gx", "gy", None),
            P(),
            P(),
            P(),
            P(),
        ),
        out_specs=(P(None, "gx", "gy", None), P(None, "gx", "gy", None), P(), P(), P(), P()),
        check_vma=False,
    )
```

```python
import functools
import math

import jax
import jax.numpy as jnp
from jax import lax
from jax.experimental import pallas as pl
from jax.experimental.pallas import tpu as pltpu
from jax.sharding import PartitionSpec as P

Q = 19
HID = 64
T = 24
ONE = 19
W = 128

velocities = (
    (0, 0, 0),
    (1, 0, 0),
    (-1, 0, 0),
    (0, 1, 0),
    (0, -1, 0),
    (0, 0, 1),
    (0, 0, -1),
    (1, 1, 0),
    (-1, -1, 0),
    (1, -1, 0),
    (-1, 1, 0),
    (1, 0, 1),
    (-1, 0, -1),
    (1, 0, -1),
    (-1, 0, 1),
    (0, 1, 1),
    (0, -1, -1),
    (0, 1, -1),
    (0, -1, 1),
)
opposite = (0, 2, 1, 4, 3, 6, 5, 8, 7, 10, 9, 12, 11, 14, 13, 16, 15, 18, 17)

order = tuple(sorted(range(Q), key=lambda k: -velocities[k][0]))
place = {k: i for i, k in enumerate(order)}
UNITS = 2 * Q + 1
SOLID = 2 * Q


def y_pieces(way):
    pieces = []
    for plane in range(2):
        for k in range(Q):
            pieces.append((plane, place[k], 3 + way * velocities[k][1]))
        for k in range(Q):
            pieces.append((plane, Q + place[k], 2 - way * velocities[k][1]))
        pieces.append((plane, SOLID, 3))
    return pieces


Y_ROWS = 200


def split(a):
    high = a.astype(jnp.bfloat16).astype(jnp.float32)
    return high, a - high


def stack3(high, low):
    parts = [high, low, high]
    if (3 * high.shape[0]) % 16:
        parts.append(jnp.zeros((8, high.shape[1]), jnp.float32))
    return jnp.concatenate(parts, axis=0).astype(jnp.bfloat16)


def weights3(a):
    high, low = split(a)
    parts = [high, high, low]
    if (3 * a.shape[1]) % 16:
        parts.append(jnp.zeros((a.shape[0], 8), jnp.float32))
    return jnp.concatenate(parts, axis=1)


def weights2(a):
    high, low = split(a)
    top = jnp.concatenate([high, high], axis=1)
    bottom = jnp.concatenate([low, jnp.zeros_like(low)], axis=1)
    return jnp.concatenate([top, bottom], axis=0)


def mm2(weights, parts):
    both = mm(weights, jnp.concatenate(parts, axis=0).astype(jnp.bfloat16))
    return both[0:T] + both[T:]


def mm(a, b):
    return lax.dot_general(a, b, (((1,), (0,)), ((), ())), preferred_element_type=jnp.float32)


def mm_t(a, b):
    return lax.dot_general(a, b, (((1,), (1,)), ((), ())), preferred_element_type=jnp.float32)


def load_rows(ref, plane, first, count):
    return jnp.concatenate(
        [ref[plane, (first + i) * T : (first + i + 1) * T, :] for i in range(count)], axis=1
    )


def store_rows(ref, plane, first, count, value):
    for i in range(count):
        ref[plane, (first + i) * T : (first + i + 1) * T, :] = value[:, i * W : (i + 1) * W]


def get8(ref, plane, first, k):
    return ref[plane, pl.ds(first * T + k, 8, stride=T), :]


def put8(ref, plane, first, k, value):
    ref[plane, pl.ds(first * T + k, 8, stride=T), :] = value


def z_shift(value, step):
    if step == 0:
        return value
    return pltpu.roll(value, step % W, axis=1)


def pad_tile():
    row = lax.broadcasted_iota(jnp.int32, (8, W), 0)
    return jnp.where(row == ONE - 16, 1.0, 0.0).astype(jnp.float32)


def pad_rows(ref, plane, first, count):
    tile = pad_tile()
    for i in range(count):
        ref[plane, (first + i) * T + 16 : (first + i + 1) * T, :] = tile


def chunks(count, size):
    return [(i, min(size, count - i)) for i in range(0, count, size)]


def first_kernel(
    start_hbm, adjoint_hbm, solid_hbm, w_in_t_hbm, b_in_hbm, w_out_hbm, b_out_hbm,
    z, to_even, to_odd, s0, w1x, w2x, w2tx, w1tx, b2b,
    p1, sq, start, adjoint, solid, w_in_t, b_in, w_out, b_out, sems,
):
    pairs = (
        (w_in_t_hbm, w_in_t), (b_in_hbm, b_in), (w_out_hbm, w_out), (b_out_hbm, b_out),
        (start_hbm, start), (solid_hbm, solid), (adjoint_hbm, adjoint),
    )
    copies = [pltpu.make_async_copy(a, b, sems.at[i]) for i, (a, b) in enumerate(pairs)]
    for copy in copies:
        copy.start()
    sq[...] = jnp.zeros((128, 128), jnp.float32)
    for plane in range(2):
        pad_rows(s0, plane, 0, 8)
    for copy in copies[:4]:
        copy.wait()
    sq[0:Q, 0:HID] = w_in_t[...]
    sq[ONE : ONE + 1, 0:HID] = b_in[...]
    a1t = sq[0:T, 0:HID]
    a1 = sq[...].T[0:HID, 0:T]
    sq[...] = jnp.zeros((128, 128), jnp.float32)
    sq[0:Q, 0:HID] = w_out[...]
    a2 = sq[0:T, 0:HID]
    a2t = sq[...].T[0:HID, 0:T]
    sq[...] = jnp.zeros((128, 128), jnp.float32)
    sq[0:1, 0:Q] = b_out[...]
    b2 = jnp.broadcast_to(sq[...].T[0:T, 0:1], (T, W))
    w1 = weights3(a1)
    w2 = weights2(a2)
    w1x[...] = w1
    w2x[...] = w2
    w2tx[...] = weights3(a2t)
    w1tx[...] = weights2(a1t)
    b2b[...] = b2
    w1 = w1.astype(jnp.bfloat16)
    w2 = w2.astype(jnp.bfloat16)
    for copy in copies[4:]:
        copy.wait()
    for plane in range(2):
        for k in range(Q):
            put8(s0, plane, 0, k, start[k, plane])
        sol = solid[plane].astype(jnp.float32)
        z[plane, SOLID] = sol
        mask = sol > 0.5
        for k in range(Q):
            z[plane, Q + place[k]] = jnp.where(
                mask, adjoint[opposite[k], plane], adjoint[k, plane]
            )
    state = jnp.concatenate([load_rows(s0, plane, 0, 8) for plane in range(2)], axis=1)
    hidden = jnp.tanh(mm(w1, stack3(*split(state))))
    change = mm2(w2, split(hidden))
    for i in range(16):
        plane, y = divmod(i, 8)
        fluid = 1.0 - solid[plane, y : y + 1, :].astype(jnp.float32)
        p1[plane, y * T : (y + 1) * T, :] = state[:, i * W : (i + 1) * W] + fluid * (
            change[:, i * W : (i + 1) * W] + b2
        )
    for plane in range(2):
        for k in range(Q):
            z[plane, place[k]] = get8(p1, plane, 0, k)

    def pack(ref, way):
        at = 0
        for plane, unit, rows in y_pieces(way):
            begin = 8 - rows if way == 1 else 0
            ref[at : at + rows, :] = z[plane, unit, begin : begin + rows, :]
            at += rows
        ref[at:, :] = jnp.zeros((Y_ROWS - at, W), jnp.float32)

    odd = lax.rem(lax.axis_index("gy"), 2)

    @pl.when(odd == 0)
    def _():
        pack(to_even, 1)
        pack(to_odd, -1)

    @pl.when(odd == 1)
    def _():
        pack(to_even, -1)
        pack(to_odd, 1)


def near_kernel(z_own, z):
    z[...] = z_own[...]


def second_kernel(z_own, from_even, from_odd, z, next_rows, to_near, to_far):
    z[:, :, 4:12, :] = z_own[...]

    def unpack(below, above):
        for ref, way in ((below, 1), (above, -1)):
            at = 0
            for plane, unit, rows in y_pieces(way):
                begin = 4 - rows if way == 1 else 12
                z[plane, unit, begin : begin + rows, :] = ref[at : at + rows, :]
                at += rows
        next_rows[OWN : OWN + Y_ROWS, :] = below[...]
        next_rows[OWN + Y_ROWS :, :] = above[...]

    for plane in range(2):
        for unit in range(UNITS):
            at = (plane * UNITS + unit) * 8
            next_rows[at : at + 8, :] = z_own[plane, unit]

    odd = lax.rem(lax.axis_index("gy"), 2)

    @pl.when(odd == 0)
    def _():
        unpack(from_odd, from_even)

    @pl.when(odd == 1)
    def _():
        unpack(from_even, from_odd)

    def pack(ref, way):
        at = 0
        for plane, unit, begin, rows in far_pieces(way):
            ref[at : at + rows, :] = z[plane, unit, begin : begin + rows, :]
            at += rows
        ref[at:, :] = jnp.zeros((FAR_ROWS - at, W), jnp.float32)

    low = lax.rem(lax.axis_index("gx"), 4) < 2

    @pl.when(low)
    def _():
        pack(to_near, 1)
        pack(to_far, -1)

    @pl.when(jnp.logical_not(low))
    def _():
        pack(to_near, -1)
        pack(to_far, 1)


def far_runs(way):
    if way == 1:
        return ((5, 0, 0), (14, 1, 0), (5, 1, Q + 14), (1, 1, SOLID))
    return ((5, 1, 14), (14, 0, 5), (5, 0, Q), (1, 0, SOLID))


def far_pieces(way):
    below = {piece[:2]: piece[2] for piece in y_pieces(1)}
    above = {piece[:2]: piece[2] for piece in y_pieces(-1)}
    units = [(plane, first + i) for count, plane, first in far_runs(way) for i in range(count)]
    pieces = [(plane, unit, 4, 8) for plane, unit in units]
    for key in units:
        pieces.append((*key, 4 - below[key], below[key]))
        pieces.append((*key, 12, above[key]))
    return pieces


FAR_ROWS = 344
OWN = 2 * UNITS * 8


def hold_kernel(f_far, z_odd, token):
    del f_far, z_odd
    token[...] = jnp.zeros(token.shape, jnp.float32)


PLANES = 10
ROWS = 16


def third_kernel(
    scale,
    s0, z_own, z_even, z_odd, f_near, f_far, w1x, w2x, w2tx, w1tx, b2b, token,
    final_hbm, grad_hbm, sums,
    packed, final, grad, out_sems, zs, s1, p2, s2, p3, gp, g, acc1, acc2, sems,
):
    index = lax.axis_index("gx")
    odd = lax.rem(index, 2)
    low = lax.rem(index, 4) < 2
    del token
    copies = [(z_even, zs.at[pl.ds(6 - 4 * odd, 2)]), (z_own, zs.at[4:6])]
    copies = [pltpu.make_async_copy(a, b, sems.at[i]) for i, (a, b) in enumerate(copies)]
    for copy in copies:
        copy.start()

    w1 = w1x[...].astype(jnp.bfloat16)
    w2 = w2x[...].astype(jnp.bfloat16)
    w2t = w2tx[...].astype(jnp.bfloat16)
    w1t = w1tx[...].astype(jnp.bfloat16)
    b2 = b2b[...]
    acc1[...] = jnp.zeros(acc1.shape, jnp.float32)
    acc2[...] = jnp.zeros(acc2.shape, jnp.float32)
    for ref, planes in ((s1, 8), (s2, 6)):
        for plane in range(planes):
            pad_rows(ref, plane, 0, ROWS)
    for plane in range(6):
        for i in range(ROWS):
            gp[plane, i * T + 16 : (i + 1) * T, :] = jnp.zeros((8, W), jnp.float32)

    for plane in range(2):
        for unit in range(UNITS):
            at = (plane * UNITS + unit) * 8
            zs[2 + 4 * odd + plane, unit, 4:12, :] = z_odd[at : at + 8, :]
    for way, at in ((1, OWN), (-1, OWN + Y_ROWS)):
        for plane, unit, count in y_pieces(way):
            begin = 4 - count if way == 1 else 12
            zs[2 + 4 * odd + plane, unit, begin : begin + count, :] = z_odd[at : at + count, :]
            at += count

    def unpack(left, right):
        for ref, way, base in ((left, 1, 0), (right, -1, 8)):
            at = 0
            for plane, unit, begin, count in far_pieces(way):
                zs[base + plane, unit, begin : begin + count, :] = ref[at : at + count, :]
                at += count

    @pl.when(low)
    def _():
        unpack(f_far, f_near)

    @pl.when(jnp.logical_not(low))
    def _():
        unpack(f_near, f_far)

    for copy in copies:
        copy.wait()

    def fluid_rows(x, y):
        return 1.0 - zs[x, SOLID, y : y + 1, :]

    def forward_hidden(state_parts):
        return jnp.tanh(mm(w1, stack3(*state_parts)))

    def collide(p_ref, p_plane, zx, first, count, state, hidden_parts):
        change = mm2(w2, hidden_parts)
        for i in range(count):
            y = first + i
            p_ref[p_plane, y * T : (y + 1) * T, :] = state[:, i * W : (i + 1) * W] + fluid_rows(
                zx, y
            ) * (change[:, i * W : (i + 1) * W] + b2)

    def backward(own, zx, first, count, state_parts, hidden, hidden_parts, grad_post):
        change = jnp.concatenate(
            [
                fluid_rows(zx, first + i) * grad_post[:, i * W : (i + 1) * W]
                for i in range(count)
            ],
            axis=1,
        )
        change_parts = split(change)
        grad_hidden = mm(w2t, stack3(*change_parts))
        grad_pre = grad_hidden * (1.0 - hidden * hidden)
        pre_parts = split(grad_pre)
        back = grad_post + mm2(w1t, pre_parts)
        low = max(first, 4)
        high = min(first + count, 12)

        if own and high > low:
            part = slice((low - first) * W, (high - first) * W)
            left = jnp.concatenate([a[:, part] for a in state_parts], axis=0)
            right = jnp.concatenate([a[:, part] for a in pre_parts + change_parts], axis=0)
            acc1[...] += mm_t(left.astype(jnp.bfloat16), right.astype(jnp.bfloat16))
            left = jnp.concatenate([a[:, part] for a in change_parts], axis=0)
            right = jnp.concatenate([a[:, part] for a in hidden_parts], axis=0)
            acc2[...] += mm_t(left.astype(jnp.bfloat16), right.astype(jnp.bfloat16))
        return back

    def over_planes(halo, body):
        if halo:
            lax.fori_loop(
                0,
                2 * halo,
                lambda i, c: body(False, jnp.where(i < halo, i, i + 2), c),
                0,
                unroll=2 * halo,
            )
        lax.fori_loop(0, 2, lambda i, c: body(True, i + halo, c), 0, unroll=2)

    def reflect(values, mask):
        return [jnp.where(mask, values[opposite[k]], values[k]) for k in range(Q)]

    def stage1(j, carry):
        zx = j + 1
        for y in (1, 7):
            moved = []
            for k in range(Q):
                cx, cy, cz = velocities[k]
                moved.append(z_shift(zs[zx - cx, place[k], y - cy : y - cy + 8, :], cz))
            moved = reflect(moved, zs[zx, SOLID, y : y + 8, :] > 0.5)
            for k in range(Q):
                put8(s1, j, y, k, moved[k])
        for first, count in chunks(14, 14):
            first += 1
            state = load_rows(s1, j, first, count)
            hidden = forward_hidden(split(state))
            collide(p2, j, zx, first, count, state, split(hidden))
        return carry

    lax.fori_loop(0, 8, stage1, 0, unroll=8)

    def stage2(own, j, carry):
        zx = j + 2
        for y in (2, 6):
            moved = []
            for k in range(Q):
                cx, cy, cz = velocities[k]
                moved.append(z_shift(get8(p2, j + 1 - cx, y - cy, k), cz))
            moved = reflect(moved, zs[zx, SOLID, y : y + 8, :] > 0.5)
            for k in range(Q):
                put8(s2, j, y, k, moved[k])
            for k in range(Q):
                cx, cy, cz = velocities[k]
                value = zs[zx + cx, Q + place[k], y + cy : y + cy + 8, :]
                put8(gp, j, y, k, z_shift(value, -cz))
        for first, count in chunks(12, 12):
            first += 2
            state = load_rows(s2, j, first, count)
            state_parts = split(state)
            hidden = forward_hidden(state_parts)
            hidden_parts = split(hidden)
            collide(p3, j, zx, first, count, state, hidden_parts)
            grad_post = load_rows(gp, j, first, count)
            back = backward(own, zx, first, count, state_parts, hidden, hidden_parts, grad_post)
            store_rows(g, j, first, count, back)
        return carry

    over_planes(2, stage2)

    for plane in range(2):
        moved = []
        for k in range(Q):
            cx, cy, cz = velocities[k]
            moved.append(z_shift(get8(p3, plane + 2 - cx, 4 - cy, k), cz))
        moved = reflect(moved, zs[plane + 4, SOLID, 4:12, :] > 0.5)
        for k in range(Q):
            final[k, plane] = moved[k]
    final_copy = pltpu.make_async_copy(final, final_hbm, out_sems.at[0])
    final_copy.start()

    def run_back(g_ref, g_plane, zx, y, out_plane):
        for k in range(Q):
            cx, cy, cz = velocities[k]
            one = get8(g_ref, g_plane + cx, y + cy, k)
            if k != 0:
                other = get8(g_ref, g_plane + cx, y + cy, opposite[k])
                mask = zs[zx + cx, SOLID, y + cy : y + cy + 8, :] > 0.5
                one = jnp.where(mask, other, one)
            put8(gp, out_plane, y, k, z_shift(one, -cz))

    def stage3(own, j, carry):
        zx = j + 3
        for y in (3, 5):
            run_back(g, j + 1, zx, y, j)
        for first, count in ((3, 10),):
            state_parts = split(load_rows(s1, j + 2, first, count))
            hidden = forward_hidden(state_parts)
            grad_post = load_rows(gp, j, first, count)
            back = backward(own, zx, first, count, state_parts, hidden, split(hidden), grad_post)
            store_rows(p2, j, first, count, back)
        return carry

    over_planes(1, stage3)

    def stage4(own, j, carry):
        zx = j + 4
        run_back(p2, j + 1, zx, 4, j)
        for first, count in ((4, 8),):
            state_parts = split(load_rows(s0, j, first - 4, count))
            hidden = forward_hidden(state_parts)
            grad_post = load_rows(gp, j, first, count)
            back = backward(own, zx, first, count, state_parts, hidden, split(hidden), grad_post)
            store_rows(g, j, first, count, back)
        for k in range(Q):
            grad[k, j] = get8(g, j, 4, k)
        return carry

    over_planes(0, stage4)
    grad_copy = pltpu.make_async_copy(grad, grad_hbm, out_sems.at[1])
    grad_copy.start()

    one = acc1[0:T, :] + acc1[T : 2 * T, :]
    two = acc2[0:T, :] + acc2[T : 2 * T, :]
    in_part = one[:, 0:HID] + one[:, HID : 2 * HID]
    out_part = two[:, 0:HID] + two[:, HID : 2 * HID]
    bias = one[:, 2 * HID : 2 * HID + T] + one[:, 2 * HID + T : 2 * HID + 2 * T]
    packed[...] = jnp.zeros(packed.shape, jnp.float32)
    packed[0:T, 0:HID] = in_part * scale
    packed[0:Q, HID : 2 * HID] = out_part[0:Q, :] * scale
    packed[ONE : ONE + 1, HID : HID + T] = bias[ONE : ONE + 1, :] * scale
    for i in range(ONE + 1):
        sums[i] = packed[i : i + 1, :]
    final_copy.wait()
    grad_copy.wait()


def last_kernel(parts, grad_w_in_t, grad_b_in, grad_w_out, grad_b_out):
    for row in range(ONE + 1):
        total = parts[0, row]
        for i in range(1, parts.shape[0]):
            total = total + parts[i, row]
        if row < Q:
            grad_w_in_t[row : row + 1, :] = total[:, 0:HID]
            grad_w_out[row : row + 1, :] = total[:, HID : 2 * HID]
        else:
            grad_b_in[...] = total[:, 0:HID]
            grad_b_out[...] = total[:, HID : HID + Q]


def swap_even(x, axis, step=1):
    count = lax.axis_size(axis)
    return lax.ppermute(x, axis, [(i, i ^ step) for i in range(count)])


def swap_odd(x, axis, step=1):
    count = lax.axis_size(axis)
    return lax.ppermute(
        x, axis, [(i, (i + step if i & step else i - step) % count) for i in range(count)]
    )


def spread(x, groups):
    count = len(groups[0])
    return lax.all_to_all(
        jnp.broadcast_to(x[None], (count,) + x.shape), ("gx", "gy"), 0, 0, axis_index_groups=groups
    )


def sum_groups():
    gx, gy = lax.axis_size("gx"), lax.axis_size("gy")
    nx, ny = math.gcd(gx, 8), math.gcd(gy, 8)
    zs = [(a, b) for b in range(gy // ny) for a in range(gx // nx)]

    def at(z, x, y):
        return (z[0] * nx + x) * gy + z[1] * ny + y

    return (
        [[at(z, x, y) for x in range(nx)] for z in zs for y in range(ny)],
        [[at(z, x, y) for z in zs] for x in range(nx) for y in range(ny)],
        [[at(z, x, y) for y in range(ny)] for z in zs for x in range(nx)],
    )


F32 = jnp.float32


def shape(*dims):
    return jax.ShapeDtypeStruct(dims, F32)


FIRST_VMEM = 63 * 1024 * 1024
PARAMS = pltpu.CompilerParams(vmem_limit_bytes=48 * 1024 * 1024)


def on_device(start, adjoint, solid, w_in, b_in, w_out, b_out):
    rows = pltpu.VMEM
    z, to_even, to_odd, s0, w1x, w2x, w2tx, w1tx, b2b = pl.pallas_call(
        first_kernel,
        out_shape=(
            shape(2, UNITS, 8, W),
            shape(Y_ROWS, W),
            shape(Y_ROWS, W),
            shape(2, 8 * T, W),
            shape(HID, 80),
            shape(2 * T, 2 * HID),
            shape(HID, 80),
            shape(2 * T, 2 * HID),
            shape(T, W),
        ),
        in_specs=[pl.BlockSpec(memory_space=pltpu.HBM)] * 7,
        scratch_shapes=[
            rows((2, 8 * T, W), F32),
            rows((128, 128), F32),
            rows((Q, 2, 8, W), F32),
            rows((Q, 2, 8, W), F32),
            rows((2, 8, W), jnp.int32),
            rows((Q, HID), F32),
            rows((1, HID), F32),
            rows((Q, HID), F32),
            rows((1, Q), F32),
            pltpu.SemaphoreType.DMA((7,)),
        ],
        compiler_params=pltpu.CompilerParams(vmem_limit_bytes=FIRST_VMEM),
        name="first",
    )(start, adjoint, solid, w_in.T, b_in.reshape(1, HID), w_out, b_out.reshape(1, Q))

    from_even = swap_even(to_even, "gy")
    from_odd = swap_odd(to_odd, "gy")

    z = pl.pallas_call(
        near_kernel,
        out_shape=shape(2, UNITS, 8, W),
        compiler_params=PARAMS,
        name="near",
    )(z)
    z, next_rows, to_near, to_far = pl.pallas_call(
        second_kernel,
        out_shape=(
            shape(2, UNITS, ROWS, W),
            shape(OWN + 2 * Y_ROWS, W),
            shape(FAR_ROWS, W),
            shape(FAR_ROWS, W),
        ),
        compiler_params=PARAMS,
        name="second",
    )(z, from_even, from_odd)

    z_odd = swap_odd(next_rows, "gx")
    f_far = swap_odd(to_far, "gx", 2)
    f_near = swap_even(to_near, "gx", 2)
    z_even = swap_even(z, "gx")

    token = pl.pallas_call(
        hold_kernel,
        out_shape=shape(8, W),
        in_specs=[pl.BlockSpec(memory_space=pl.ANY)] * 2,
        compiler_params=PARAMS,
        cost_estimate=pl.CostEstimate(flops=6 * 10**9, bytes_accessed=10**6, transcendentals=0),
        name="hold",
    )(f_far, z_odd)

    cells = 16 * W * lax.axis_size("gx") * lax.axis_size("gy")
    vmem = pl.BlockSpec(memory_space=pltpu.VMEM)
    hbm = pl.BlockSpec(memory_space=pl.ANY)
    final, grad, sums = pl.pallas_call(
        functools.partial(third_kernel, 1.0 / math.sqrt(cells)),
        out_shape=(shape(Q, 2, 8, W), shape(Q, 2, 8, W), shape(ONE + 1, 1, W)),
        in_specs=[vmem] + [hbm] * 2 + [vmem] * 8 + [hbm],
        out_specs=(hbm, hbm, vmem),
        scratch_shapes=[
            rows((T, W), F32),
            rows((Q, 2, 8, W), F32),
            rows((Q, 2, 8, W), F32),
            pltpu.SemaphoreType.DMA((2,)),
            rows((PLANES, UNITS, ROWS, W), F32),
            rows((8, ROWS * T, W), F32),
            rows((8, ROWS * T, W), F32),
            rows((6, ROWS * T, W), F32),
            rows((6, ROWS * T, W), F32),
            rows((6, ROWS * T, W), F32),
            rows((6, ROWS * T, W), F32),
            rows((2 * T, 2 * HID + 2 * T), F32),
            rows((2 * T, 2 * HID), F32),
            pltpu.SemaphoreType.DMA((2,)),
        ],
        compiler_params=PARAMS,
        name="third",
    )(s0, z, z_even, z_odd, f_near, f_far, w1x, w2x, w2tx, w1tx, b2b, token)

    along_x, along_z, along_y = sum_groups()
    sums = spread(sums, along_y).sum(0)
    sums = spread(sums, along_z).sum(0)
    grad_w_in_t, grad_b_in, grad_w_out, grad_b_out = pl.pallas_call(
        last_kernel,
        out_shape=(shape(Q, HID), shape(1, HID), shape(Q, HID), shape(1, Q)),
        compiler_params=PARAMS,
        name="last",
    )(spread(sums, along_x))
    return final, grad, grad_w_in_t.T, grad_b_in[0], grad_w_out, grad_b_out[0]


def solution(mesh):
    return jax.shard_map(
        on_device,
        mesh=mesh,
        in_specs=(
            P(None, "gx", "gy", None),
            P(None, "gx", "gy", None),
            P("gx", "gy", None),
            P(),
            P(),
            P(),
            P(),
        ),
        out_specs=(P(None, "gx", "gy", None), P(None, "gx", "gy", None), P(), P(), P(), P()),
        check_vma=False,
    )
```
